512 devices in a mesh: rows: 64 (over z, x), dims: 8 (over y, core).
Axes of the slice: x: 4, y: 4, z: 16, core: 2. Of those that a mesh axis runs over, the one named last changes fastest.
Arguments:
- noise_latents: bfloat16 [8192, 32768], P('rows', 'dims'), may hold values from -6 to 6
- data_latents: bfloat16 [1536, 32768], P('rows', 'dims'), may hold values from -6 to 6
Outputs:
- targets: bfloat16 [8192, 32768], P('rows', 'dims')
- column_potential: float32 [1536], replicated
The draws below stay inside these ranges and needn't reach their ends.
All inputs are finite; a program needn't handle non-finite values.
Results may differ from the reference program's by a relative error of at most 0.0054.
Values may be sent and summed in bfloat16 or wider, within the bound.
A program may use at most 64 MiB of HBM per device.

```python
import math
import jax
import jax.numpy as jnp
from jax import lax

D = 32768
ROWS_DEV = 128
ITERS = 3
NOISE = 8192
DATA = 1536
N_ROWS = 64


def levels(stream_key, shape, pieces, least, largest):
    gain, own = 1.0, jax.random.fold_in(stream_key, 6)
    for axis_at, shards_of in pieces:
        heights = jnp.exp(jax.random.uniform(jax.random.fold_in(own, axis_at), (shards_of,), jnp.float32, least / len(pieces), largest / len(pieces)))
        gain = gain * jnp.repeat(heights, shape[axis_at] // shards_of).reshape([-1 if axis == axis_at else 1 for axis in range(len(shape))])
    return gain


def gaussian(own_key, dims, width, most, cuts=(), held_as=jnp.bfloat16):
    result = width * jax.random.normal(own_key, dims, jnp.float32)
    if cuts:
        result = result * levels(own_key, dims, cuts, -0.22, 0.18)
    return jnp.clip(result, -most, most).astype(held_as)


def setup_inputs(seed: int = 0) -> dict:
    seeds = jax.random.split(jax.random.key(seed), 3)
    return {
        "noise_latents": gaussian(seeds[0], (NOISE, D), 1.0, 6.0, ((0, 64), (1, 8))),
        "data_latents": gaussian(seeds[1], (DATA, D), 1.0, 6.0, ((0, 64), (1, 8))),
    }


def reference(noise_latents, data_latents):
    entropic = 0.4 / math.sqrt(D)
    data_wide = data_latents.astype(jnp.float32)
    data_sq = lax.optimization_barrier(jnp.sum(data_wide * data_wide, axis=1))

    def cost_block(noise_block):
        noise_wide = noise_block.astype(jnp.float32)
        products = jnp.dot(noise_wide, data_wide.T, precision=lax.Precision.HIGHEST)
        noise_sq = lax.optimization_barrier(jnp.sum(noise_wide * noise_wide, axis=1))
        return (noise_sq[:, None] + data_sq[None, :] - 2.0 * products) / D
    transport = lax.map(cost_block, noise_latents.reshape(N_ROWS, ROWS_DEV, D)).reshape(NOISE, DATA)
    log_columns = jnp.log(jnp.float32(DATA))
    log_rows = jnp.log(jnp.float32(NOISE))
    potential = jnp.zeros((DATA,), jnp.float32)
    for iteration in range(ITERS):
        row_potential = -entropic * (jax.nn.logsumexp((potential[None, :] - transport) / entropic, axis=1) - log_columns)
        potential = -entropic * (jax.nn.logsumexp((row_potential[:, None] - transport) / entropic, axis=0) - log_rows)
    weights = jax.nn.softmax((potential[None, :] - transport) / entropic, axis=1).astype(jnp.bfloat16)

    def target_block(plan_block):
        return jnp.dot(plan_block.astype(jnp.float32), data_wide, precision=lax.Precision.HIGHEST)
    targets = lax.map(target_block, weights.reshape(N_ROWS, ROWS_DEV, DATA)).reshape(NOISE, D).astype(jnp.bfloat16)
    return (targets, potential)
```

```python
import functools
import math

import jax
import jax.numpy as jnp
from jax import lax
from jax.experimental import pallas as pl
from jax.experimental.pallas import tpu as pltpu
from jax.sharding import PartitionSpec as P

ITERS = 3
NZ, NX, NY, NC = 16, 4, 4, 2
PIECES = 6
LAG = 4
NEG = -1e30
MESH = pl.DeviceIdType.MESH
F32, BF16 = jnp.float32, jnp.bfloat16


def logsumexp0(v):
    top = jnp.max(v, axis=0, keepdims=True)
    return top + jnp.log(jnp.sum(jnp.exp(v - top), axis=0, keepdims=True))


def spread(v, n):
    return jnp.transpose(jnp.broadcast_to(v, (n, n)))


def kernel(
    dims_total, x_ref, y_ref, t_ref, pot_ref,
    ysend, yr, xg, yg, x2, part, cx, sm, rs, a1, a2, pb, rbuf, zbuf, xbuf, pbuf, wt, tst,
    y_s, y_r, x_s, x_r, own_sem, ring_s, ring_r, core_s, core_r, sum_s, sum_r,
    row_s, row_r, cz_s, cz_r, cx_s, cx_r, pot_s, pot_r, w_s, w_r, wf_s, wf_r, t_s, t_r, to_sem,
):
    rows_dev, width = x_ref.shape
    quarter = width // NX
    half = quarter // 2
    block_rows = NX * 24
    own_rows = block_rows // NC
    main_rows = NX * 16
    nq = NZ // NY
    mine = nq * own_rows
    padded = a1.shape[0]
    piece = block_rows // PIECES
    columns = NZ * block_rows
    noise = NZ * NX * rows_dev
    entropic = 0.4 / math.sqrt(dims_total)

    r_id, d_id = lax.axis_index("rows"), lax.axis_index("dims")
    z, x = r_id // NX, lax.rem(r_id, NX)
    y, c = d_id // NC, lax.rem(d_id, NC)
    other = NC - 1 - c
    me_xy = x * NY + y

    def at(x_, y_, z_, c_):
        return (z_ * NX + x_, y_ * NC + c_)

    def copy(src, dst, send, recv, to):
        return pltpu.make_async_remote_copy(
            src_ref=src, dst_ref=dst, send_sem=send, recv_sem=recv, device_id=to, device_id_type=MESH
        )

    here = at(x, y, z, c)

    def xy_peer(o):
        return lax.rem(x + o // NY, NX), lax.rem(y + lax.rem(o, NY), NY)

    barrier = pltpu.get_barrier_semaphore()

    def greet(to):
        pl.semaphore_signal(barrier, inc=1, device_id=to, device_id_type=MESH)

    def greet_xy(o, _):
        xt, yt = xy_peer(o)
        greet(at(xt, yt, z, c))
        return 0

    def greet_z(o, _):
        greet(at(x, y, lax.rem(z + o, NZ), c))
        return 0

    def greet_other(o, _):
        greet(at(x, lax.rem(y + o, NY), z, other))
        return 0

    lax.fori_loop(1, NX * NY, greet_xy, 0)
    lax.fori_loop(1, NZ, greet_z, 0)
    lax.fori_loop(0, NY, greet_other, 0)

    wide = y_ref[...].astype(F32)
    for q in range(NX):
        lo = wide[16:24, q * quarter : q * quarter + half]
        hi = wide[16:24, q * quarter + half : (q + 1) * quarter]
        ysend[q, :, 0:quarter] = wide[0:16, q * quarter : (q + 1) * quarter].astype(BF16)
        ysend[q, :, quarter:] = jnp.concatenate([lo, hi], axis=0).astype(BF16)

    pl.semaphore_wait(barrier, (NX * NY - 1) + (NZ - 1) + NY)

    def y_copy(o):
        xt = lax.rem(x + o, NX)
        return copy(ysend.at[xt], yr.at[x], y_s.at[o - 1], y_r.at[o - 1], at(xt, y, z, c))

    def x_copy(o):
        xt = lax.rem(x + o, NX)
        cols = pl.ds(pl.multiple_of(xt * quarter, quarter), quarter)
        return copy(x_ref.at[:, cols], xg.at[x], x_s.at[o - 1], x_r.at[o - 1], at(xt, y, z, c))

    for o in range(1, NX):
        y_copy(o).start()
    for o in range(1, NX):
        x_copy(o).start()
    own_x = pltpu.make_async_copy(
        x_ref.at[:, pl.ds(pl.multiple_of(x * quarter, quarter), quarter)], xg.at[x], own_sem.at[0]
    )
    own_x.start()
    yr[x] = ysend[x]
    for o in range(1, NX):
        y_copy(o).wait()

    def slot(z_):
        return lax.rem(z_, NY) * nq + z_ // NY

    mid = slot(z)
    tails = []
    for s in range(NX):
        yg[mid, s * 16 : (s + 1) * 16, :] = yr[s, :, 0:quarter]
        tail = yr[s, :, quarter:].astype(F32)
        tails.append(jnp.concatenate([tail[0:8], tail[8:16]], axis=1))
    yg[mid, main_rows:block_rows, :] = jnp.concatenate(tails, axis=0).astype(BF16)

    def ring_copy(way, step, u, z_):
        rows = pl.ds(pl.multiple_of(u * piece, piece), piece)
        ref = yg.at[slot(z_), rows]
        to = lax.rem(z + 1, NZ) if way == 0 else lax.rem(z + NZ - 1, NZ)
        return copy(ref, ref, ring_s.at[way, step - 1, u], ring_r.at[way, step - 1, u], at(x, y, to, c))

    def origin(way, step):
        return lax.rem(z + NZ - step, NZ) if way == 0 else lax.rem(z + step, NZ)

    last = NZ // 2

    def ring_first(u, _):
        for way in range(2):
            ring_copy(way, 1, u, z).start()
        return 0

    lax.fori_loop(0, PIECES, ring_first, 0)

    def pass_on(step, u):
        for way in range(2):
            ring_copy(way, step, u, origin(way, step)).wait_recv()

            @pl.when((step < last - 1) | ((u < PIECES // 2) == (way == 0)))
            def _():
                ring_copy(way, step + 1, u, origin(way, step)).start()

    def source(b):
        away = (b + 1) // 2
        return lax.rem(jnp.where(lax.rem(b, 2) == 1, z + away, z + NZ - away), NZ)

    def core_copy(s):
        return copy(part.at[s, other], cx.at[s], core_s.at[s], core_r.at[s], at(x, y, z, other))

    def distance(b):
        s = slot(source(b))
        rows = yg[s]
        noise_block = xg[...].reshape(NX * rows_dev, quarter)
        products = lax.dot_general(rows, noise_block, (((1,), (1,)), ((), ())), preferred_element_type=F32)
        tall = rows.astype(F32)
        data_sq = jnp.sum(tall * tall, axis=1, keepdims=True)
        value = (x2[0:1, :] + data_sq - 2.0 * products) * (1.0 / dims_total)
        for k in range(NC):
            part[s, k] = value[k * own_rows : (k + 1) * own_rows]
        core_copy(s).start()

    def sum_copy(s, o, zs):
        xt = lax.rem(x + o, NX)
        return copy(
            sm.at[s, xt], rs.at[me_xy, zs // NY], sum_s.at[s, o], sum_r.at[me_xy, zs // NY],
            at(xt, lax.rem(zs, NY), z, c),
        )

    def hand_out(b):
        zs = source(b)
        s = slot(zs)
        core_copy(s).wait()
        value = part[s, c] + cx[s]
        for k in range(NX):
            sm[s, k] = value[:, k * rows_dev : (k + 1) * rows_dev]
        for o in range(1, NX):
            sum_copy(s, o, zs).start()

        @pl.when(lax.rem(zs, NY) == y)
        def _():
            rs[me_xy, zs // NY] = sm[s, x]

        @pl.when(lax.rem(zs, NY) != y)
        def _():
            sum_copy(s, 0, zs).start()

    def early(step, _):
        def each(u, _):
            pass_on(step, u)
            return 0

        return lax.fori_loop(0, PIECES, each, 0)

    lax.fori_loop(1, LAG, early, 0)

    own_x.wait()
    for o in range(1, NX):
        x_copy(o).wait()
    for s in range(NX):
        tall = xg[s].astype(F32)
        norm = jnp.sum(tall * tall, axis=1, keepdims=True)
        flat = jnp.transpose(jnp.broadcast_to(norm, (rows_dev, rows_dev)))
        x2[:, s * rows_dev : (s + 1) * rows_dev] = flat[0:8]

    blocks = NZ - 1
    per = PIECES // 2

    def work(step, i):
        b = (step - LAG) * per + i

        @pl.when(b < blocks)
        def _():
            distance(b)

        @pl.when((b >= per) & (b - per < blocks))
        def _():
            hand_out(b - per)

    def later(step, _):
        def each(i, _):
            pass_on(step, 2 * i)
            pass_on(step, 2 * i + 1)
            work(step, i)
            return 0

        return lax.fori_loop(0, per, each, 0)

    lax.fori_loop(LAG, last, later, 0)
    far = lax.rem(z + last, NZ)

    def ring_last(i, _):
        ring_copy(0, last, i, far).wait_recv()
        ring_copy(1, last, i + per, far).wait_recv()
        work(last, i)
        return 0

    lax.fori_loop(0, per, ring_last, 0)
    done = (last + 1 - LAG) * per

    def rest(b, _):
        hand_out(b)
        return 0

    def rest_distance(b, _):
        distance(b)
        return 0

    lax.fori_loop(min(done, blocks), blocks, rest_distance, 0)
    lax.fori_loop(min(done - per, blocks), blocks, rest, 0)
    distance(NZ - 1)

    def ring_sent(step, _):
        def each(u, _):
            for way in range(2):
                @pl.when((step < last) | ((u < PIECES // 2) == (way == 0)))
                def _():
                    ring_copy(way, step, u, z).wait_send()
            return 0

        return lax.fori_loop(0, PIECES, each, 0)

    lax.fori_loop(1, last + 1, ring_sent, 0)
    hand_out(NZ - 1)

    def sums_sent(zs, _):
        for o in range(1, NX):
            sum_copy(slot(zs), o, zs).wait_send()

        @pl.when(lax.rem(zs, NY) != y)
        def _():
            sum_copy(slot(zs), 0, zs).wait_send()

        return 0

    lax.fori_loop(0, NZ, sums_sent, 0)

    def sums_in(src, _):
        @pl.when(src != me_xy)
        def _():
            for q in range(nq):
                copy(rs.at[src, q], rs.at[src, q], sum_s.at[0, 0], sum_r.at[src, q], here).wait_recv()

        return 0

    lax.fori_loop(0, NX * NY, sums_in, 0)
    for q in range(nq):
        total = rs[0, q]
        for src in range(1, NX * NY):
            total = total + rs[src, q]
        a1[q * own_rows : (q + 1) * own_rows, :] = total * (-1.0 / entropic)
    if padded > mine:
        a1[mine:padded, :] = jnp.full((padded - mine, rows_dev), NEG, F32)
    for h in range(padded // rows_dev):
        cut = slice(h * rows_dev, (h + 1) * rows_dev)
        a2[:, cut] = jnp.transpose(a1[cut, :])
    pb[...] = jnp.zeros_like(pb)

    def exchange(buf, it, me, n, peer, send, recv):
        def desc(i, who):
            return copy(buf.at[it, who], buf.at[it, who], send.at[it, i - 1], recv.at[it, i - 1], peer(lax.rem(me + i, n)))

        def begin(i, _):
            desc(i, me).start()
            return 0

        def sent(i, _):
            desc(i, me).wait_send()
            return 0

        def end(i, _):
            desc(i, lax.rem(me + n - i, n)).wait_recv()
            return 0

        lax.fori_loop(1, n, begin, 0)
        lax.fori_loop(1, n, sent, 0)
        lax.fori_loop(1, n, end, 0)
        return logsumexp0(buf[it])[0]

    def yc_peer(k):
        return at(x, k // NC, z, lax.rem(k, NC))

    def row_total(it):
        rbuf[it, d_id] = logsumexp0(a1[...] + pb[...])
        return exchange(rbuf, it, d_id, NY * NC, yc_peer, row_s, row_r)

    real = lax.broadcasted_iota(jnp.int32, (1, padded), 1) < mine

    def iteration(it, _):
        row = spread(math.log(columns) - row_total(it), rows_dev)
        for h in range(padded // rows_dev):
            cut = slice(h * rows_dev, (h + 1) * rows_dev)
            zbuf[it, z, :, cut] = logsumexp0(a2[:, cut] + row)
        xbuf[it, x] = exchange(zbuf, it, z, NZ, lambda k: at(x, y, k, c), cz_s, cz_r)
        total = exchange(xbuf, it, x, NX, lambda k: at(k, y, z, c), cx_s, cx_r)
        p = jnp.where(real, math.log(noise) - total, 0.0)
        pbuf[0, d_id] = p
        for h in range(padded // rows_dev):
            cut = slice(h * rows_dev, (h + 1) * rows_dev)
            pb[cut, :] = spread(p[:, cut], rows_dev)
        return 0

    lax.fori_loop(0, ITERS, iteration, 0)

    def pot_copy(i, who):
        return copy(
            pbuf.at[0, who], pbuf.at[0, who], pot_s.at[i - 1], pot_r.at[i - 1], yc_peer(lax.rem(d_id + i, NY * NC))
        )

    def pot_begin(i, _):
        pot_copy(i, d_id).start()
        return 0

    norm = row_total(ITERS)
    lax.fori_loop(1, NY * NC, pot_begin, 0)
    weights = jnp.exp(a1[0:mine, :] + pb[0:mine, :] - norm)
    wt[x, y, :, c] = weights.reshape(nq, own_rows, rows_dev).astype(BF16)

    def w_copy(o, xs, ys):
        xt, yt = xy_peer(o)
        ref = wt.at[xs, ys, :, c]
        return copy(ref, ref, w_s.at[o - 1], w_r.at[o - 1], at(xt, yt, z, c))

    def w_begin(o, _):
        w_copy(o, x, y).start()
        return 0

    lax.fori_loop(1, NX * NY, w_begin, 0)

    def wf_copy(o, core):
        ref = wt.at[lax.rem(x + o, NX), :, :, core]
        return copy(ref, ref, wf_s.at[o], wf_r.at[o], at(x, y, z, other))

    def relay(i, _):
        o = NX - 1 - i
        xs = lax.rem(x + o, NX)
        back = lax.rem(NX - o, NX)

        def arrive(dy, _):
            k = back * NY + dy

            @pl.when(k > 0)
            def _():
                w_copy(k, xs, lax.rem(y + NY - dy, NY)).wait_recv()

            return 0

        lax.fori_loop(0, NY, arrive, 0)
        wf_copy(o, c).start()
        return 0

    def t_copy(o):
        xt = lax.rem(x + o, NX)
        cols = pl.ds(pl.multiple_of(x * quarter, quarter), quarter)
        return copy(tst.at[o], t_ref.at[:, cols], t_s.at[o], t_r.at[o], at(xt, y, z, c))

    own_t = pltpu.make_async_copy(
        tst.at[0], t_ref.at[:, pl.ds(pl.multiple_of(x * quarter, quarter), quarter)], to_sem.at[0]
    )

    def target(i, _):
        o = NX - 1 - i
        xs = lax.rem(x + o, NX)
        wf_copy(o, other).wait_recv()
        w = wt[xs].reshape(columns, rows_dev)
        value = lax.dot_general(
            w, yg[...].reshape(columns, quarter), (((0,), (0,)), ((), ())), preferred_element_type=F32
        )
        tst[o] = value.astype(BF16)

        @pl.when(o > 0)
        def _():
            t_copy(o).start()

        @pl.when(o == 0)
        def _():
            own_t.start()

        return 0

    lax.fori_loop(0, NX, relay, 0)
    lax.fori_loop(0, NX, target, 0)

    def w_sent(o, _):
        w_copy(o, x, y).wait_send()
        return 0

    lax.fori_loop(1, NX * NY, w_sent, 0)

    def wf_sent(o, _):
        wf_copy(o, c).wait_send()
        return 0

    lax.fori_loop(0, NX, wf_sent, 0)

    def pot_end(i, _):
        pot_copy(i, d_id).wait_send()
        pot_copy(i, lax.rem(d_id + NY * NC - i, NY * NC)).wait_recv()
        return 0

    lax.fori_loop(1, NY * NC, pot_end, 0)
    pot_ref[...] = pbuf[0] * entropic
    own_t.wait()
    for o in range(1, NX):
        t_copy(o).wait()


def on_device(noise_latents, data_latents):
    rows_dev, width = noise_latents.shape
    quarter = width // NX
    block_rows = NX * 24
    own_rows = block_rows // NC
    nq = NZ // NY
    mine = nq * own_rows
    padded = -(-mine // rows_dev) * rows_dev
    nd = NY * NC
    dma = pltpu.SemaphoreType.DMA
    last = NZ // 2
    sems = [
        (NX - 1,), (NX - 1,), (NX - 1,), (NX - 1,), (1,),
        (2, last, PIECES), (2, last, PIECES), (NZ,), (NZ,), (NZ, NX), (NX * NY, nq),
        (ITERS + 1, nd - 1), (ITERS + 1, nd - 1), (ITERS, NZ - 1), (ITERS, NZ - 1), (ITERS, NX - 1), (ITERS, NX - 1),
        (nd - 1,), (nd - 1,), (NX * NY - 1,), (NX * NY - 1,), (NX,), (NX,), (NX,), (NX,), (1,),
    ]
    targets, pots = pl.pallas_call(
        functools.partial(kernel, width * nd),
        out_shape=(
            jax.ShapeDtypeStruct((rows_dev, width), BF16),
            jax.ShapeDtypeStruct((nd, 1, padded), F32),
        ),
        in_specs=[pl.BlockSpec(memory_space=pl.ANY), pl.BlockSpec(memory_space=pltpu.VMEM)],
        out_specs=(pl.BlockSpec(memory_space=pl.ANY), pl.BlockSpec(memory_space=pltpu.VMEM)),
        scratch_shapes=[
            pltpu.VMEM((NX, 16, quarter * 3 // 2), BF16),
            pltpu.VMEM((NX, 16, quarter * 3 // 2), BF16),
            pltpu.VMEM((NX, rows_dev, quarter), BF16),
            pltpu.VMEM((NZ, block_rows, quarter), BF16),
            pltpu.VMEM((8, NX * rows_dev), F32),
            pltpu.VMEM((NZ, NC, own_rows, NX * rows_dev), F32),
            pltpu.VMEM((NZ, own_rows, NX * rows_dev), F32),
            pltpu.VMEM((NZ, NX, own_rows, rows_dev), F32),
            pltpu.VMEM((NX * NY, nq, own_rows, rows_dev), F32),
            pltpu.VMEM((padded, rows_dev), F32),
            pltpu.VMEM((rows_dev, padded), F32),
            pltpu.VMEM((padded, rows_dev), F32),
            pltpu.VMEM((ITERS + 1, nd, 1, rows_dev), F32),
            pltpu.VMEM((ITERS, NZ, 1, padded), F32),
            pltpu.VMEM((ITERS, NX, 1, padded), F32),
            pltpu.VMEM((1, nd, 1, padded), F32),
            pltpu.VMEM((NX, NY, nq, NC, own_rows, rows_dev), BF16),
            pltpu.VMEM((NX, rows_dev, quarter), BF16),
        ]
        + [dma(shape) for shape in sems],
        compiler_params=pltpu.CompilerParams(
            collective_id=0, has_side_effects=True, vmem_limit_bytes=48 * 1024 * 1024
        ),
    )(noise_latents, data_latents)
    flat = pots[:, 0, :mine].reshape(NY, NC, nq, own_rows).transpose(2, 0, 1, 3).reshape(NZ, block_rows)
    main = flat[:, : NX * 16].reshape(NZ, NX, 16)
    tail = flat[:, NX * 16 :].reshape(NZ, NX, 8)
    return targets, jnp.concatenate([main, tail], axis=2).reshape(-1)


def solution(mesh):
    placed = (P("rows", "dims"), P("rows", "dims"))
    return jax.shard_map(
        on_device, mesh=mesh, in_specs=placed, out_specs=(P("rows", "dims"), P()), check_vma=False
    )
```

```python
import functools
import math

import jax
import jax.numpy as jnp
from jax import lax
from jax.experimental import pallas as pl
from jax.experimental.pallas import tpu as pltpu
from jax.sharding import PartitionSpec as P

ITERS = 3
NZ, NX, NY, NC = 16, 4, 4, 2
PIECES = 6
LAG = 3
NEG = -1e30
MESH = pl.DeviceIdType.MESH
F32, BF16 = jnp.float32, jnp.bfloat16


def logsumexp0(v):
    top = jnp.max(v, axis=0, keepdims=True)
    return top + jnp.log(jnp.sum(jnp.exp(v - top), axis=0, keepdims=True))


def spread(v, n):
    return jnp.transpose(jnp.broadcast_to(v, (n, n)))


def kernel(
    dims_total, x_ref, y_ref, t_ref, pot_ref,
    ybuf, ysend, yr, xg, yg, x2, part, cx, sm, rs, a1, a2, pb, rbuf, zbuf, xbuf, pbuf, full, pall, wt, tst,
    y_s, y_r, x_s, x_r, own_sem, ring_s, ring_r, core_s, core_r, sum_s, sum_r,
    row_s, row_r, cz_s, cz_r, cx_s, cx_r, pot_s, pot_r, one_s, one_r, set_s, set_r, core2_s, core2_r, t_s, t_r, to_sem,
):
    rows_dev, width = x_ref.shape
    quarter = width // NX
    half = quarter // 2
    block_rows = NX * 24
    own_rows = block_rows // NC
    nq = NZ // NY
    mine = nq * own_rows
    padded = a1.shape[0]
    piece = block_rows // PIECES
    columns = NZ * block_rows
    noise = NZ * NX * rows_dev
    entropic = 0.4 / math.sqrt(dims_total)

    r_id, d_id = lax.axis_index("rows"), lax.axis_index("dims")
    z, x = r_id // NX, lax.rem(r_id, NX)
    y, c = d_id // NC, lax.rem(d_id, NC)
    other = NC - 1 - c
    me_xy = x * NY + y

    def at(x_, y_, z_, c_):
        return (z_ * NX + x_, y_ * NC + c_)

    def copy(src, dst, send, recv, to):
        return pltpu.make_async_remote_copy(
            src_ref=src, dst_ref=dst, send_sem=send, recv_sem=recv, device_id=to, device_id_type=MESH
        )

    here = at(x, y, z, c)

    def xy_peer(o):
        return lax.rem(x + o // NY, NX), lax.rem(y + lax.rem(o, NY), NY)

    fetch = pltpu.make_async_copy(y_ref, ybuf, own_sem.at[1])
    fetch.start()

    barrier = pltpu.get_barrier_semaphore()

    def greet(to):
        pl.semaphore_signal(barrier, inc=1, device_id=to, device_id_type=MESH)

    for o in range(1, NX):
        greet(at(lax.rem(x + o, NX), y, z, c))
    for o in range(1, NY):
        greet(at(x, lax.rem(y + o, NY), z, c))
    greet(at(x, y, lax.rem(z + 1, NZ), c))
    greet(at(x, y, lax.rem(z + NZ - 1, NZ), c))
    greet(at(x, y, z, other))

    fetch.wait()
    wide = ybuf[...].astype(F32)
    for q in range(NX):
        lo = wide[16:24, q * quarter : q * quarter + half]
        hi = wide[16:24, q * quarter + half : (q + 1) * quarter]
        ysend[q, :, 0:quarter] = wide[0:16, q * quarter : (q + 1) * quarter].astype(BF16)
        ysend[q, :, quarter:] = jnp.concatenate([lo, hi], axis=0).astype(BF16)

    pl.semaphore_wait(barrier, (NX - 1) + (NY - 1) + 2 + 1)

    def y_copy(o):
        xt = lax.rem(x + o, NX)
        return copy(ysend.at[xt], yr.at[x], y_s.at[o - 1], y_r.at[o - 1], at(xt, y, z, c))

    def x_copy(o):
        xt = lax.rem(x + o, NX)
        cols = pl.ds(pl.multiple_of(xt * quarter, quarter), quarter)
        return copy(x_ref.at[:, cols], xg.at[x], x_s.at[o - 1], x_r.at[o - 1], at(xt, y, z, c))

    for o in range(1, NX):
        y_copy(o).start()
    for o in range(1, NX):
        x_copy(o).start()
    own_x = pltpu.make_async_copy(
        x_ref.at[:, pl.ds(pl.multiple_of(x * quarter, quarter), quarter)], xg.at[x], own_sem.at[0]
    )
    own_x.start()
    yr[x] = ysend[x]
    for o in range(1, NX):
        y_copy(o).wait()

    def slot(z_):
        return lax.rem(z_, NY) * nq + z_ // NY

    mid = slot(z)
    pieces = []
    for k in range(NX):
        rows = yr[k].astype(F32)
        pieces.append(rows[:, 0:quarter])
        pieces.append(jnp.concatenate([rows[0:8, quarter:], rows[8:16, quarter:]], axis=1))
    yg[mid] = jnp.concatenate(pieces, axis=0).astype(BF16)

    def ring_copy(way, step, u, z_):
        rows = pl.ds(pl.multiple_of(u * piece, piece), piece)
        ref = yg.at[slot(z_), rows]
        to = lax.rem(z + 1, NZ) if way == 0 else lax.rem(z + NZ - 1, NZ)
        return copy(ref, ref, ring_s.at[way, step - 1, u], ring_r.at[way, step - 1, u], at(x, y, to, c))

    def origin(way, step):
        return lax.rem(z + NZ - step, NZ) if way == 0 else lax.rem(z + step, NZ)

    last = NZ // 2

    def ring_first(u, _):
        for way in range(2):
            ring_copy(way, 1, u, z).start()
        return 0

    lax.fori_loop(0, PIECES, ring_first, 0)

    def pass_on(step, u):
        for way in range(2):
            ring_copy(way, step, u, origin(way, step)).wait_recv()

            @pl.when((step < last - 1) | ((u < PIECES // 2) == (way == 0)))
            def _():
                ring_copy(way, step + 1, u, origin(way, step)).start()

    def source(b):
        away = (b + 1) // 2
        return lax.rem(jnp.where(lax.rem(b, 2) == 1, z + away, z + NZ - away), NZ)

    def core_copy(s):
        return copy(part.at[s, other], cx.at[s], core_s.at[s], core_r.at[s], at(x, y, z, other))

    def distance(b):
        s = slot(source(b))
        rows = yg[s]
        noise_block = xg[...].reshape(NX * rows_dev, quarter)
        products = lax.dot_general(rows, noise_block, (((1,), (1,)), ((), ())), preferred_element_type=F32)
        tall = rows.astype(F32)
        data_sq = jnp.sum(tall * tall, axis=1, keepdims=True)
        value = (x2[0:1, :] + data_sq - 2.0 * products) * (1.0 / dims_total)
        for k in range(NC):
            part[s, k] = value[k * own_rows : (k + 1) * own_rows]
        core_copy(s).start()

    def sum_copy(s, o, zs):
        xt = lax.rem(x + o, NX)
        return copy(
            sm.at[s, xt], rs.at[me_xy, zs // NY], sum_s.at[s, o], sum_r.at[me_xy, zs // NY],
            at(xt, lax.rem(zs, NY), z, c),
        )

    def hand_out(b):
        zs = source(b)
        s = slot(zs)
        core_copy(s).wait()
        value = part[s, c] + cx[s]
        for k in range(NX):
            sm[s, k] = value[:, k * rows_dev : (k + 1) * rows_dev]
        for o in range(1, NX):
            sum_copy(s, o, zs).start()

        @pl.when(lax.rem(zs, NY) == y)
        def _():
            rs[me_xy, zs // NY] = sm[s, x]

        @pl.when(lax.rem(zs, NY) != y)
        def _():
            sum_copy(s, 0, zs).start()

    def early(step, _):
        def each(u, _):
            pass_on(step, u)
            return 0

        return lax.fori_loop(0, PIECES, each, 0)

    lax.fori_loop(1, LAG, early, 0)

    own_x.wait()
    for o in range(1, NX):
        x_copy(o).wait()
    for s in range(NX):
        tall = xg[s].astype(F32)
        norm = jnp.sum(tall * tall, axis=1, keepdims=True)
        flat = jnp.transpose(jnp.broadcast_to(norm, (rows_dev, rows_dev)))
        x2[:, s * rows_dev : (s + 1) * rows_dev] = flat[0:8]

    blocks = NZ - 1
    per = PIECES // 2

    def work(step, i):
        b = (step - LAG) * per + i - 1

        @pl.when((b >= 0) & (b < blocks))
        def _():
            distance(b)

        @pl.when((b >= per) & (b - per < blocks))
        def _():
            hand_out(b - per)

    def later(step, _):
        def each(i, _):
            pass_on(step, 2 * i)
            pass_on(step, 2 * i + 1)
            work(step, i)
            return 0

        return lax.fori_loop(0, per, each, 0)

    lax.fori_loop(LAG, last, later, 0)
    far = lax.rem(z + last, NZ)

    def ring_last(i, _):
        ring_copy(0, last, i, far).wait_recv()
        ring_copy(1, last, i + per, far).wait_recv()
        work(last, i)
        return 0

    lax.fori_loop(0, per, ring_last, 0)
    done = (last + 1 - LAG) * per - 1

    def rest(b, _):
        hand_out(b)
        return 0

    def rest_distance(b, _):
        distance(b)
        return 0

    lax.fori_loop(min(done, blocks), blocks, rest_distance, 0)
    lax.fori_loop(max(min(done - per, blocks), 0), blocks, rest, 0)
    distance(NZ - 1)

    def ring_sent(step, _):
        def each(u, _):
            for way in range(2):
                @pl.when((step < last) | ((u < PIECES // 2) == (way == 0)))
                def _():
                    ring_copy(way, step, u, z).wait_send()
            return 0

        return lax.fori_loop(0, PIECES, each, 0)

    lax.fori_loop(1, last + 1, ring_sent, 0)
    hand_out(NZ - 1)

    def sums_sent(zs, _):
        for o in range(1, NX):
            sum_copy(slot(zs), o, zs).wait_send()

        @pl.when(lax.rem(zs, NY) != y)
        def _():
            sum_copy(slot(zs), 0, zs).wait_send()

        return 0

    lax.fori_loop(0, NZ, sums_sent, 0)

    def sums_in(src, _):
        @pl.when(src != me_xy)
        def _():
            for q in range(nq):
                copy(rs.at[src, q], rs.at[src, q], sum_s.at[0, 0], sum_r.at[src, q], here).wait_recv()

        return 0

    lax.fori_loop(0, NX * NY, sums_in, 0)
    for q in range(nq):
        total = rs[0, q]
        for src in range(1, NX * NY):
            total = total + rs[src, q]
        a1[q * own_rows : (q + 1) * own_rows, :] = total * (-1.0 / entropic)
    if padded > mine:
        a1[mine:padded, :] = jnp.full((padded - mine, rows_dev), NEG, F32)
    for h in range(padded // rows_dev):
        cut = slice(h * rows_dev, (h + 1) * rows_dev)
        a2[:, cut] = jnp.transpose(a1[cut, :])
    pb[...] = jnp.zeros_like(pb)

    def exchange(buf, it, me, n, peer, send, recv, beside=lambda: None):
        def desc(i, who):
            return copy(buf.at[it, who], buf.at[it, who], send.at[it, i - 1], recv.at[it, i - 1], peer(lax.rem(me + i, n)))

        def begin(i, _):
            desc(i, me).start()
            return 0

        def sent(i, _):
            desc(i, me).wait_send()
            return 0

        def end(i, _):
            desc(i, lax.rem(me + n - i, n)).wait_recv()
            return 0

        lax.fori_loop(1, n, begin, 0)
        beside()
        lax.fori_loop(1, n, sent, 0)
        lax.fori_loop(1, n, end, 0)
        return buf[it]

    def yc_peer(k):
        return at(x, k // NC, z, lax.rem(k, NC))

    def row_total(it):
        rbuf[it, d_id] = logsumexp0(a1[...] + pb[...])
        return logsumexp0(exchange(rbuf, it, d_id, NY * NC, yc_peer, row_s, row_r))[0]

    full[c, x, y] = a1[0:mine, :]
    plane = ((NY, y, NX, x), (NX, x, NY, y))

    def peer_of(core, along_first, o):
        if (core == 0) == along_first:
            return at(x, lax.rem(y + o, NY), z, c)
        return at(lax.rem(x + o, NX), y, z, c)

    def one_copy(core, o, back):
        n, pos = plane[core][0:2]
        src = lax.rem(pos + n - o, n) if back else pos
        ref = full.at[0, x, src] if core == 0 else full.at[1, src, y]
        return copy(ref, ref, one_s.at[o - 1], one_r.at[o - 1], peer_of(core, True, o))

    def set_ref(core, o):
        n, pos = plane[core][2:4]
        src = lax.rem(pos + n - o, n)
        return full.at[0, src] if core == 0 else full.at[1, :, src]

    def set_copy(core, o, back):
        ref = set_ref(core, o if back else 0)
        return copy(ref, ref, set_s.at[o - 1], set_r.at[o - 1], peer_of(core, False, o))

    def over_copy(core, o):
        ref = set_ref(core, o)
        return copy(ref, ref, core2_s.at[o], core2_r.at[o], at(x, y, z, other))

    def by_core(step):
        for core in range(NC):
            @pl.when(c == core)
            def _():
                step(core)

    def near(n):
        return sorted({1, n - 1})

    def distant(n):
        return range(2, n - 1)

    def first_part(core):
        for o in range(1, plane[core][0]):
            one_copy(core, o, False).start()

    def second_part(core):
        for o in range(1, plane[core][0]):
            one_copy(core, o, True).wait_recv()
        for o in near(plane[core][2]):
            set_copy(core, o, False).start()
        over_copy(core, 0).start()

    def third_part(core):
        for o in distant(plane[core][2]):
            set_copy(core, o, False).start()
        for o in near(plane[core][2]):
            set_copy(core, o, True).wait_recv()
            over_copy(core, o).start()

    def last_part(core):
        for o in distant(plane[core][2]):
            set_copy(core, o, True).wait_recv()
            over_copy(core, o).start()

    def all_in(core):
        for o in range(plane[1 - core][2]):
            over_copy(1 - core, o).wait_recv()

    def all_out(core):
        for o in range(1, plane[core][0]):
            one_copy(core, o, False).wait_send()
        for o in range(1, plane[core][2]):
            set_copy(core, o, False).wait_send()
        for o in range(plane[core][2]):
            over_copy(core, o).wait_send()

    def spread_scores(it):
        for k, part_of in enumerate((first_part, second_part, third_part)):
            @pl.when(it == k)
            def _():
                by_core(part_of)

    real = lax.broadcasted_iota(jnp.int32, (1, padded), 1) < mine

    def columns_along_z(it):
        row = spread(math.log(columns) - row_total(it), rows_dev)
        for h in range(padded // rows_dev):
            cut = slice(h * rows_dev, (h + 1) * rows_dev)
            zbuf[it, z, :, cut] = logsumexp0(a2[:, cut] + row)
        return logsumexp0(
            exchange(zbuf, it, z, NZ, lambda k: at(x, y, k, c), cz_s, cz_r, lambda: spread_scores(it))
        )[0]

    def iteration(it, _):
        xbuf[it, x] = columns_along_z(it)
        total = logsumexp0(exchange(xbuf, it, x, NX, lambda k: at(k, y, z, c), cx_s, cx_r))[0]
        p = jnp.where(real, math.log(noise) - total, 0.0)
        for h in range(padded // rows_dev):
            cut = slice(h * rows_dev, (h + 1) * rows_dev)
            pb[cut, :] = spread(p[:, cut], rows_dev)
        return 0

    lax.fori_loop(0, ITERS - 1, iteration, 0)

    me_plane = x * NY * NC + d_id
    pbuf[0, me_plane] = columns_along_z(ITERS - 1)
    found = exchange(
        pbuf, 0, me_plane, NX * NY * NC, lambda k: (z * NX + k // (NY * NC), lax.rem(k, NY * NC)),
        pot_s, pot_r, lambda: by_core(last_part),
    )
    pots = math.log(noise) - logsumexp0(found.reshape(NX, NY * NC, 1, padded))[0]
    pot_ref[...] = pots * entropic
    for k in range(NY * NC):
        for h in range(padded // rows_dev):
            lo, hi = h * rows_dev, min((h + 1) * rows_dev, mine)
            pall[k % NC * NY + k // NC, lo:hi, :] = spread(pots[k, :, lo : lo + rows_dev], rows_dev)[0 : hi - lo]

    by_core(all_in)

    def t_copy(o):
        xt = lax.rem(x + o, NX)
        cols = pl.ds(pl.multiple_of(x * quarter, quarter), quarter)
        return copy(tst.at[o], t_ref.at[:, cols], t_s.at[o], t_r.at[o], at(xt, y, z, c))

    own_t = pltpu.make_async_copy(
        tst.at[0], t_ref.at[:, pl.ds(pl.multiple_of(x * quarter, quarter), quarter)], to_sem.at[0]
    )

    def target(i, _):
        o = lax.rem(NX // 2 + i, NX)
        xs = lax.rem(x + o, NX)
        scores = jnp.concatenate([full[k, xs] for k in range(NC)], axis=0) + pall[...]
        top = jnp.max(jnp.max(scores, axis=0), axis=0, keepdims=True)
        powers = jnp.exp(scores - top)
        weights = powers * (1.0 / jnp.sum(jnp.sum(powers, axis=0), axis=0, keepdims=True))
        for k in range(NY * NC):
            wt[k % NY, :, k // NY] = weights[k].reshape(nq, own_rows, rows_dev).astype(BF16)
        w = wt[...].reshape(columns, rows_dev)
        value = lax.dot_general(
            w, yg[...].reshape(columns, quarter), (((0,), (0,)), ((), ())), preferred_element_type=F32
        )
        tst[o] = value.astype(BF16)

        @pl.when(o > 0)
        def _():
            t_copy(o).start()

        @pl.when(o == 0)
        def _():
            own_t.start()

        return 0

    lax.fori_loop(0, NX, target, 0)

    by_core(all_out)
    own_t.wait()
    for o in range(1, NX):
        t_copy(o).wait()


def on_device(noise_latents, data_latents):
    rows_dev, width = noise_latents.shape
    quarter = width // NX
    block_rows = NX * 24
    own_rows = block_rows // NC
    nq = NZ // NY
    mine = nq * own_rows
    padded = -(-mine // rows_dev) * rows_dev
    nd = NY * NC
    dma = pltpu.SemaphoreType.DMA
    last = NZ // 2
    longest = max(NX, NY)
    sems = [
        (NX - 1,), (NX - 1,), (NX - 1,), (NX - 1,), (2,),
        (2, last, PIECES), (2, last, PIECES), (NZ,), (NZ,), (NZ, NX), (NX * NY, nq),
        (ITERS, nd - 1), (ITERS, nd - 1), (ITERS, NZ - 1), (ITERS, NZ - 1), (ITERS - 1, NX - 1), (ITERS - 1, NX - 1),
        (1, NX * nd - 1), (1, NX * nd - 1),
        (longest,), (longest,), (longest,), (longest,), (longest,), (longest,), (NX,), (NX,), (1,),
    ]
    targets, pots = pl.pallas_call(
        functools.partial(kernel, width * nd),
        out_shape=(
            jax.ShapeDtypeStruct((rows_dev, width), BF16),
            jax.ShapeDtypeStruct((nd, 1, padded), F32),
        ),
        in_specs=[pl.BlockSpec(memory_space=pl.ANY)] * 2,
        out_specs=(pl.BlockSpec(memory_space=pl.ANY), pl.BlockSpec(memory_space=pltpu.VMEM)),
        scratch_shapes=[
            pltpu.VMEM(data_latents.shape, BF16),
            pltpu.VMEM((NX, 16, quarter * 3 // 2), BF16),
            pltpu.VMEM((NX, 16, quarter * 3 // 2), BF16),
            pltpu.VMEM((NX, rows_dev, quarter), BF16),
            pltpu.VMEM((NZ, block_rows, quarter), BF16),
            pltpu.VMEM((8, NX * rows_dev), F32),
            pltpu.VMEM((NZ, NC, own_rows, NX * rows_dev), F32),
            pltpu.VMEM((NZ, own_rows, NX * rows_dev), F32),
            pltpu.VMEM((NZ, NX, own_rows, rows_dev), F32),
            pltpu.VMEM((NX * NY, nq, own_rows, rows_dev), F32),
            pltpu.VMEM((padded, rows_dev), F32),
            pltpu.VMEM((rows_dev, padded), F32),
            pltpu.VMEM((padded, rows_dev), F32),
            pltpu.VMEM((ITERS, nd, 1, rows_dev), F32),
            pltpu.VMEM((ITERS, NZ, 1, padded), F32),
            pltpu.VMEM((ITERS - 1, NX, 1, padded), F32),
            pltpu.VMEM((1, NX * nd, 1, padded), F32),
            pltpu.VMEM((NC, NX, NY, mine, rows_dev), F32),
            pltpu.VMEM((nd, mine, rows_dev), F32),
            pltpu.VMEM((NY, nq, NC, own_rows, rows_dev), BF16),
            pltpu.VMEM((NX, rows_dev, quarter), BF16),
        ]
        + [dma(shape) for shape in sems],
        compiler_params=pltpu.CompilerParams(
            collective_id=0, has_side_effects=True, vmem_limit_bytes=60 * 1024 * 1024
        ),
    )(noise_latents, data_latents)
    flat = pots[:, 0, :mine].reshape(NY, NC, nq, own_rows).transpose(2, 0, 1, 3)
    return targets, flat.reshape(-1)


def solution(mesh):
    placed = (P("rows", "dims"), P("rows", "dims"))
    return jax.shard_map(
        on_device, mesh=mesh, in_specs=placed, out_specs=(P("rows", "dims"), P()), check_vma=False
    )
```

```python
import functools
import math

import jax
import jax.numpy as jnp
from jax import lax
from jax.experimental import pallas as pl
from jax.experimental.pallas import tpu as pltpu
from jax.sharding import PartitionSpec as P

ITERS = 3
NZ, NX, NY, NC = 16, 4, 4, 2
PIECES = 6
SPLIT = 1
LAG = 3
NEG = -1e30
MESH = pl.DeviceIdType.MESH
F32, BF16 = jnp.float32, jnp.bfloat16


def logsumexp0(v):
    top = jnp.max(v, axis=0, keepdims=True)
    return top + jnp.log(jnp.sum(jnp.exp(v - top), axis=0, keepdims=True))


def spread(v, n):
    return jnp.transpose(jnp.broadcast_to(v, (n, n)))


def kernel(
    dims_total, x_ref, y_ref, t_ref, pot_ref,
    ybuf, ysend, yr, xg, yg, x2, part, cx, sm, rs, a1, a2, pb, rbuf, zbuf, xbuf, pbuf, full, pall, wt, tst,
    y_s, y_r, x_s, x_r, own_sem, ring_s, ring_r, core_s, core_r, sum_s, sum_r,
    row_s, row_r, cz_s, cz_r, cx_s, cx_r, pot_s, pot_r, one_s, one_r, set_s, set_r, core2_s, core2_r, t_s, t_r,
):
    rows_dev, width = x_ref.shape
    quarter = width // NX
    half = quarter // 2
    block_rows = NX * 24
    own_rows = block_rows // NC
    pairs = NY // SPLIT
    nq = NZ // pairs
    share = own_rows // SPLIT
    mine = nq * share
    padded = a1.shape[0]
    piece = block_rows // PIECES
    columns = NZ * block_rows
    noise = NZ * NX * rows_dev
    entropic = 0.4 / math.sqrt(dims_total)

    r_id, d_id = lax.axis_index("rows"), lax.axis_index("dims")
    z, x = r_id // NX, lax.rem(r_id, NX)
    y, c = d_id // NC, lax.rem(d_id, NC)
    other = NC - 1 - c
    me_xy = x * NY + y

    def at(x_, y_, z_, c_):
        return (z_ * NX + x_, y_ * NC + c_)

    def copy(src, dst, send, recv, to):
        return pltpu.make_async_remote_copy(
            src_ref=src, dst_ref=dst, send_sem=send, recv_sem=recv, device_id=to, device_id_type=MESH
        )

    here = at(x, y, z, c)

    def xy_peer(o):
        return lax.rem(x + o // NY, NX), lax.rem(y + lax.rem(o, NY), NY)

    fetch = pltpu.make_async_copy(y_ref, ybuf, own_sem.at[1])
    fetch.start()

    barrier = pltpu.get_barrier_semaphore()

    def greet(to):
        pl.semaphore_signal(barrier, inc=1, device_id=to, device_id_type=MESH)

    for o in range(1, NX):
        greet(at(lax.rem(x + o, NX), y, z, c))
    for o in range(1, NY):
        greet(at(x, lax.rem(y + o, NY), z, c))
    greet(at(x, y, lax.rem(z + 1, NZ), c))
    greet(at(x, y, lax.rem(z + NZ - 1, NZ), c))
    greet(at(x, y, z, other))

    fetch.wait()
    wide = ybuf[...].astype(F32)
    for q in range(NX):
        lo = wide[16:24, q * quarter : q * quarter + half]
        hi = wide[16:24, q * quarter + half : (q + 1) * quarter]
        ysend[q, :, 0:quarter] = wide[0:16, q * quarter : (q + 1) * quarter].astype(BF16)
        ysend[q, :, quarter:] = jnp.concatenate([lo, hi], axis=0).astype(BF16)

    pl.semaphore_wait(barrier, (NX - 1) + (NY - 1) + 2 + 1)

    def y_copy(o):
        xt = lax.rem(x + o, NX)
        return copy(ysend.at[xt], yr.at[x], y_s.at[o - 1], y_r.at[o - 1], at(xt, y, z, c))

    x_piece = 16

    def x_copy(o, k=None):
        xt = lax.rem(x + o, NX)
        cols = pl.ds(pl.multiple_of(xt * quarter, quarter), quarter)
        rows = pl.ds(0, rows_dev) if k is None else pl.ds(k * x_piece, x_piece)
        return copy(x_ref.at[rows, cols], xg.at[x, rows], x_s.at[o - 1], x_r.at[o - 1], at(xt, y, z, c))

    for o in range(1, NX):
        y_copy(o).start()
    own_x = pltpu.make_async_copy(
        x_ref.at[:, pl.ds(pl.multiple_of(x * quarter, quarter), quarter)], xg.at[x], own_sem.at[0]
    )
    own_x.start()
    yr[x] = ysend[x]
    for o in range(1, NX):
        y_copy(o).wait()

    mid = z
    pieces = []
    for k in range(NX):
        rows = yr[k].astype(F32)
        pieces.append(rows[:, 0:quarter])
        pieces.append(jnp.concatenate([rows[0:8, quarter:], rows[8:16, quarter:]], axis=1))
    yg[mid] = jnp.concatenate(pieces, axis=0).astype(BF16)

    ahead = (at(x, y, lax.rem(z + 1, NZ), c), at(x, y, lax.rem(z + NZ - 1, NZ), c))

    def ring_copy(way, step, u, place):
        ref = yg.at[place, pl.ds(pl.multiple_of(u * piece, piece), piece)]
        return copy(ref, ref, ring_s.at[way, step - 1, u], ring_r.at[way, step - 1, u], ahead[way])

    def origins(step):
        return lax.rem(z + NZ - step, NZ), lax.rem(z + step, NZ)

    last = NZ // 2

    def ring_first(u, _):
        for way in range(2):
            ring_copy(way, 1, u, mid).start()
        return 0

    lax.fori_loop(0, PIECES, ring_first, 0)

    def pass_on(step, u, places, ways=(0, 1)):
        for way in range(2):
            ring_copy(way, step, u, places[way]).wait_recv()
            if way in ways:
                ring_copy(way, step + 1, u, places[way]).start()

    def source(b):
        away = (b + 1) // 2
        return lax.rem(jnp.where(lax.rem(b, 2) == 1, z + away, z + NZ - away), NZ)

    def core_copy(s):
        return copy(part.at[s, other], cx.at[s], core_s.at[s], core_r.at[s], at(x, y, z, other))

    def distance(b):
        s = source(b)
        rows = yg[s]
        noise_block = xg[...].reshape(NX * rows_dev, quarter)
        products = lax.dot_general(rows, noise_block, (((1,), (1,)), ((), ())), preferred_element_type=F32)
        tall = rows.astype(F32)
        data_sq = jnp.sum(tall * tall, axis=1, keepdims=True)
        value = (x2[0:1, :] + data_sq - 2.0 * products) * (1.0 / dims_total)
        for k in range(NC):
            part[s, k] = value[k * own_rows : (k + 1) * own_rows]
        core_copy(s).start()

    def sum_copy(zs, o, h):
        xt, q = lax.rem(x + o, NX), zs // pairs
        return copy(
            sm.at[zs, xt, h], rs.at[me_xy, q], sum_s.at[zs, o, h], sum_r.at[me_xy, q],
            at(xt, SPLIT * lax.rem(zs, pairs) + h, z, c),
        )

    def hand_out(b):
        zs = source(b)
        core_copy(zs).wait()
        value = part[zs, c] + cx[zs]
        for k in range(NX):
            for h in range(SPLIT):
                sm[zs, k, h] = value[h * share : (h + 1) * share, k * rows_dev : (k + 1) * rows_dev]
        for o in range(1, NX):
            for h in range(SPLIT):
                sum_copy(zs, o, h).start()
        for h in range(SPLIT):
            @pl.when(SPLIT * lax.rem(zs, pairs) + h == y)
            def _():
                rs[me_xy, zs // pairs] = sm[zs, x, h]

            @pl.when(SPLIT * lax.rem(zs, pairs) + h != y)
            def _():
                sum_copy(zs, 0, h).start()

    x_turns = rows_dev // x_piece
    for k in range(max(x_turns, (LAG - 1) * PIECES)):
        if k < x_turns:
            for o in range(1, NX):
                x_copy(o, k).start()
        if k < (LAG - 1) * PIECES:
            pass_on(1 + k // PIECES, k % PIECES, origins(1 + k // PIECES))

    own_x.wait()
    for o in range(1, NX):
        x_copy(o).wait()
    for s in range(NX):
        tall = xg[s].astype(F32)
        norm = jnp.sum(tall * tall, axis=1, keepdims=True)
        flat = jnp.transpose(jnp.broadcast_to(norm, (rows_dev, rows_dev)))
        x2[:, s * rows_dev : (s + 1) * rows_dev] = flat[0:8]

    blocks = NZ - 1
    per = PIECES // 2

    def work(step, i):
        b = (step - LAG) * per + i - 1

        @pl.when((b >= 0) & (b < blocks))
        def _():
            distance(b)

        @pl.when((b >= per) & (b - per < blocks))
        def _():
            hand_out(b - per)

    def later(step, _):
        places = origins(step)

        def each(i, _):
            pass_on(step, 2 * i, places)
            pass_on(step, 2 * i + 1, places)
            work(step, i)
            return 0

        return lax.fori_loop(0, per, each, 0)

    lax.fori_loop(LAG, last - 1, later, 0)
    places = origins(last - 1)
    for i in range(per):
        for u in (2 * i, 2 * i + 1):
            pass_on(last - 1, u, places, (0,) if u < PIECES // 2 else (1,))
        work(last - 1, i)
    far = lax.rem(z + last, NZ)

    def ring_last(i, _):
        ring_copy(0, last, i, far).wait_recv()
        ring_copy(1, last, i + per, far).wait_recv()
        work(last, i)
        return 0

    lax.fori_loop(0, per, ring_last, 0)
    done = (last + 1 - LAG) * per - 1

    def rest(b, _):
        hand_out(b)
        return 0

    def rest_distance(b, _):
        distance(b)
        return 0

    lax.fori_loop(min(done, blocks), blocks, rest_distance, 0)
    distance(NZ - 1)
    lax.fori_loop(max(min(done - per, blocks), 0), blocks, rest, 0)
    hand_out(NZ - 1)

    def sum_up(b, _):
        zs = source(b)

        @pl.when(lax.rem(zs, pairs) == y // SPLIT)
        def _():
            q = zs // pairs

            def arrive(src, _):
                @pl.when(src != me_xy)
                def _():
                    copy(rs.at[src, q], rs.at[src, q], sum_s.at[0, 0, 0], sum_r.at[src, q], here).wait_recv()

                return 0

            lax.fori_loop(0, NX * NY, arrive, 0)
            total = rs[0, q]
            for src in range(1, NX * NY):
                total = total + rs[src, q]
            a1[pl.ds(pl.multiple_of(q * share, 8), share), :] = total * (-1.0 / entropic)

        return 0

    lax.fori_loop(0, NZ, sum_up, 0)

    def sent_so_far():
        def ring_sent(step, _):
            def each(u, _):
                for way in range(2):
                    @pl.when((step < last) | ((u < PIECES // 2) == (way == 0)))
                    def _():
                        ring_copy(way, step, u, mid).wait_send()
                return 0

            return lax.fori_loop(0, PIECES, each, 0)

        def sums_sent(zs, _):
            for h in range(SPLIT):
                for o in range(1, NX):
                    sum_copy(zs, o, h).wait_send()

                @pl.when(SPLIT * lax.rem(zs, pairs) + h != y)
                def _():
                    sum_copy(zs, 0, h).wait_send()

            return 0

        lax.fori_loop(1, last + 1, ring_sent, 0)
        lax.fori_loop(0, NZ, sums_sent, 0)

    if padded > mine:
        a1[mine:padded, :] = jnp.full((padded - mine, rows_dev), NEG, F32)
    for h in range(padded // rows_dev):
        cut = slice(h * rows_dev, (h + 1) * rows_dev)
        a2[:, cut] = jnp.transpose(a1[cut, :])
    pb[...] = jnp.zeros_like(pb)

    def exchange(buf, it, me, n, peer, send, recv, beside=lambda: None):
        def desc(i, who):
            return copy(buf.at[it, who], buf.at[it, who], send.at[it, i - 1], recv.at[it, i - 1], peer(lax.rem(me + i, n)))

        def begin(i, _):
            desc(i, me).start()
            return 0

        def sent(i, _):
            desc(i, me).wait_send()
            return 0

        def end(i, _):
            desc(i, lax.rem(me + n - i, n)).wait_recv()
            return 0

        lax.fori_loop(1, n, begin, 0)
        beside()
        lax.fori_loop(1, n, sent, 0)
        lax.fori_loop(1, n, end, 0)
        return buf[it]

    def yc_peer(k):
        return at(x, k // NC, z, lax.rem(k, NC))

    def row_total(it):
        rbuf[it, d_id] = logsumexp0(a1[...] + pb[...])
        return logsumexp0(exchange(rbuf, it, d_id, NY * NC, yc_peer, row_s, row_r))[0]

    full[c, x, y] = a1[0:mine, :]
    plane = ((NY, y, NX, x), (NX, x, NY, y))

    def peer_of(core, along_first, o):
        if (core == 0) == along_first:
            return at(x, lax.rem(y + o, NY), z, c)
        return at(lax.rem(x + o, NX), y, z, c)

    def one_copy(core, o, back):
        n, pos = plane[core][0:2]
        src = lax.rem(pos + n - o, n) if back else pos
        ref = full.at[0, x, src] if core == 0 else full.at[1, src, y]
        return copy(ref, ref, one_s.at[o - 1], one_r.at[o - 1], peer_of(core, True, o))

    def set_ref(core, o):
        n, pos = plane[core][2:4]
        src = lax.rem(pos + n - o, n)
        return full.at[0, src] if core == 0 else full.at[1, :, src]

    def set_copy(core, o, back):
        ref = set_ref(core, o if back else 0)
        return copy(ref, ref, set_s.at[o - 1], set_r.at[o - 1], peer_of(core, False, o))

    def over_copy(core, o):
        ref = set_ref(core, o)
        return copy(ref, ref, core2_s.at[o], core2_r.at[o], at(x, y, z, other))

    def by_core(step):
        for core in range(NC):
            @pl.when(c == core)
            def _():
                step(core)

    def near(n):
        return sorted({1, n - 1})

    def distant(n):
        return range(2, n - 1)

    def first_part(core):
        for o in range(1, plane[core][0]):
            one_copy(core, o, False).start()

    def second_part(core):
        for o in range(1, plane[core][0]):
            one_copy(core, o, True).wait_recv()
        for o in near(plane[core][2]):
            set_copy(core, o, False).start()
        over_copy(core, 0).start()

    def third_part(core):
        for o in distant(plane[core][2]):
            set_copy(core, o, False).start()
        for o in near(plane[core][2]):
            set_copy(core, o, True).wait_recv()
            over_copy(core, o).start()

    def last_part(core):
        for o in distant(plane[core][2]):
            set_copy(core, o, True).wait_recv()
            over_copy(core, o).start()

    def all_in(core):
        for o in range(plane[1 - core][2]):
            over_copy(1 - core, o).wait_recv()

    def all_out(core):
        for o in range(1, plane[core][0]):
            one_copy(core, o, False).wait_send()
        for o in range(1, plane[core][2]):
            set_copy(core, o, False).wait_send()
        for o in range(plane[core][2]):
            over_copy(core, o).wait_send()

    def spread_scores(it):
        for k, part_of in enumerate((first_part, second_part, third_part)):
            @pl.when(it == k)
            def _():
                by_core(part_of)
                if k == 0:
                    sent_so_far()

    real = lax.broadcasted_iota(jnp.int32, (1, padded), 1) < mine

    def columns_along_z(it):
        row = spread(math.log(columns) - row_total(it), rows_dev)
        for h in range(padded // rows_dev):
            cut = slice(h * rows_dev, (h + 1) * rows_dev)
            zbuf[it, z, :, cut] = logsumexp0(a2[:, cut] + row)
        return logsumexp0(
            exchange(zbuf, it, z, NZ, lambda k: at(x, y, k, c), cz_s, cz_r, lambda: spread_scores(it))
        )[0]

    def iteration(it, _):
        xbuf[it, x] = columns_along_z(it)
        total = logsumexp0(exchange(xbuf, it, x, NX, lambda k: at(k, y, z, c), cx_s, cx_r))[0]
        p = jnp.where(real, math.log(noise) - total, 0.0)
        for h in range(padded // rows_dev):
            cut = slice(h * rows_dev, (h + 1) * rows_dev)
            pb[cut, :] = spread(p[:, cut], rows_dev)
        return 0

    lax.fori_loop(0, ITERS - 1, iteration, 0)

    me_plane = x * NY * NC + d_id
    pbuf[0, me_plane] = columns_along_z(ITERS - 1)
    found = exchange(
        pbuf, 0, me_plane, NX * NY * NC, lambda k: (z * NX + k // (NY * NC), lax.rem(k, NY * NC)),
        pot_s, pot_r, lambda: by_core(last_part),
    )
    pots = math.log(noise) - logsumexp0(found.reshape(NX, NY * NC, 1, padded))[0]
    for k in range(NY * NC):
        for h in range(padded // rows_dev):
            lo, hi = h * rows_dev, min((h + 1) * rows_dev, mine)
            pall[k % NC * NY + k // NC, lo:hi, :] = spread(pots[k, :, lo : lo + rows_dev], rows_dev)[0 : hi - lo]

    by_core(all_in)

    def t_copy(o, h):
        xt = lax.rem(x + o, NX)
        cols = pl.ds(pl.multiple_of(x * quarter + h * half, half), half)
        return copy(tst.at[o, h], t_ref.at[:, cols], t_s.at[o, h], t_r.at[o, h], at(xt, y, z, c))

    def target(i, _):
        o = lax.rem(NX // 2 + i, NX)
        xs = lax.rem(x + o, NX)
        scores = jnp.concatenate([full[k, xs] for k in range(NC)], axis=0) + pall[...]
        top = jnp.max(jnp.max(scores, axis=0), axis=0, keepdims=True)
        powers = jnp.exp(scores - top)
        weights = powers * (1.0 / jnp.sum(jnp.sum(powers, axis=0), axis=0, keepdims=True))
        for k in range(NC):
            for pair in range(pairs):
                both = [weights[k * NY + SPLIT * pair + h].reshape(nq, share, rows_dev) for h in range(SPLIT)]
                wt[:, pair, k] = jnp.concatenate(both, axis=1).astype(BF16)
        w = wt[...].reshape(columns, rows_dev)
        for h in range(2):
            value = lax.dot_general(
                w, yg[:, :, h * half : (h + 1) * half].reshape(columns, half), (((0,), (0,)), ((), ())),
                preferred_element_type=F32,
            ).astype(BF16)

            @pl.when(o > 0)
            def _():
                tst[o, h] = value
                t_copy(o, h).start()

            @pl.when(o == 0)
            def _():
                t_ref[:, pl.ds(pl.multiple_of(x * quarter + h * half, half), half)] = value

        return 0

    lax.fori_loop(0, NX, target, 0)

    ordered = [
        pots[(SPLIT * pair + h) * NC + k, :, q * share : (q + 1) * share]
        for q in range(nq) for pair in range(pairs) for k in range(NC) for h in range(SPLIT)
    ]
    pot_ref[...] = (jnp.concatenate(ordered, axis=1) * entropic).reshape(columns)
    by_core(all_out)
    for o in range(1, NX):
        for h in range(2):
            t_copy(o, h).wait()


def on_device(noise_latents, data_latents):
    rows_dev, width = noise_latents.shape
    quarter = width // NX
    block_rows = NX * 24
    own_rows = block_rows // NC
    pairs = NY // SPLIT
    nq = NZ // pairs
    share = own_rows // SPLIT
    mine = nq * share
    padded = -(-mine // rows_dev) * rows_dev
    nd = NY * NC
    dma = pltpu.SemaphoreType.DMA
    last = NZ // 2
    longest = max(NX, NY)
    sems = [
        (NX - 1,), (NX - 1,), (NX - 1,), (NX - 1,), (2,),
        (2, last, PIECES), (2, last, PIECES), (NZ,), (NZ,), (NZ, NX, SPLIT), (NX * NY, nq),
        (ITERS, nd - 1), (ITERS, nd - 1), (ITERS, NZ - 1), (ITERS, NZ - 1), (ITERS - 1, NX - 1), (ITERS - 1, NX - 1),
        (1, NX * nd - 1), (1, NX * nd - 1),
        (longest,), (longest,), (longest,), (longest,), (longest,), (longest,), (NX, 2), (NX, 2),
    ]
    targets, pots = pl.pallas_call(
        functools.partial(kernel, width * nd),
        out_shape=(
            pltpu.VMEM((rows_dev, width), BF16),
            jax.ShapeDtypeStruct((NZ * block_rows,), F32),
        ),
        in_specs=[pl.BlockSpec(memory_space=pl.ANY)] * 2,
        out_specs=(pl.BlockSpec(memory_space=pltpu.VMEM),) * 2,
        scratch_shapes=[
            pltpu.VMEM(data_latents.shape, BF16),
            pltpu.VMEM((NX, 16, quarter * 3 // 2), BF16),
            pltpu.VMEM((NX, 16, quarter * 3 // 2), BF16),
            pltpu.VMEM((NX, rows_dev, quarter), BF16),
            pltpu.VMEM((NZ, block_rows, quarter), BF16),
            pltpu.VMEM((8, NX * rows_dev), F32),
            pltpu.VMEM((NZ, NC, own_rows, NX * rows_dev), F32),
            pltpu.VMEM((NZ, own_rows, NX * rows_dev), F32),
            pltpu.VMEM((NZ, NX, SPLIT, share, rows_dev), F32),
            pltpu.VMEM((NX * NY, nq, share, rows_dev), F32),
            pltpu.VMEM((padded, rows_dev), F32),
            pltpu.VMEM((rows_dev, padded), F32),
            pltpu.VMEM((padded, rows_dev), F32),
            pltpu.VMEM((ITERS, nd, 1, rows_dev), F32),
            pltpu.VMEM((ITERS, NZ, 1, padded), F32),
            pltpu.VMEM((ITERS - 1, NX, 1, padded), F32),
            pltpu.VMEM((1, NX * nd, 1, padded), F32),
            pltpu.VMEM((NC, NX, NY, mine, rows_dev), F32),
            pltpu.VMEM((nd, mine, rows_dev), F32),
            pltpu.VMEM((nq, pairs, NC, own_rows, rows_dev), BF16),
            pltpu.VMEM((NX, 2, rows_dev, quarter // 2), BF16),
        ]
        + [dma(shape) for shape in sems],
        compiler_params=pltpu.CompilerParams(
            collective_id=0, has_side_effects=True, vmem_limit_bytes=60 * 1024 * 1024
        ),
    )(noise_latents, data_latents)
    return targets, pots


def solution(mesh):
    placed = (P("rows", "dims"), P("rows", "dims"))
    return jax.shard_map(
        on_device, mesh=mesh, in_specs=placed, out_specs=(P("rows", "dims"), P()), check_vma=False
    )
```

```python
import functools
import math

import jax
import jax.numpy as jnp
from jax import lax
from jax.experimental import pallas as pl
from jax.experimental.pallas import tpu as pltpu
from jax.sharding import PartitionSpec as P

ITERS = 3
NZ, NX, NY, NC = 16, 4, 4, 2
PIECES = 6
SPLIT = 1
UNROLL = 3
LAG = 3
NEG = -1e30
MESH = pl.DeviceIdType.MESH
F32, BF16 = jnp.float32, jnp.bfloat16


def logsumexp0(v):
    top = jnp.max(v, axis=0, keepdims=True)
    return top + jnp.log(jnp.sum(jnp.exp(v - top), axis=0, keepdims=True))


def spread(v, n):
    return jnp.transpose(jnp.broadcast_to(v, (n, n)))


def kernel(
    dims_total, x_ref, y_ref, t_ref, pot_ref,
    ybuf, ysend, yr, xg, yg, x2, part, cx, sm, rs, a1, a2, pb, rbuf, zbuf, xbuf, pbuf, full, pall, wt, tst,
    y_s, y_r, x_s, x_r, own_sem, ring_s, ring_r, core_s, core_r, sum_s, sum_r,
    row_s, row_r, cz_s, cz_r, cx_s, cx_r, pot_s, pot_r, one_s, one_r, set_s, set_r, core2_s, core2_r, t_s, t_r,
):
    rows_dev, width = x_ref.shape
    quarter = width // NX
    half = quarter // 2
    block_rows = NX * 24
    own_rows = block_rows // NC
    pairs = NY // SPLIT
    nq = NZ // pairs
    share = own_rows // SPLIT
    mine = nq * share
    padded = a1.shape[0]
    piece = block_rows // PIECES
    columns = NZ * block_rows
    noise = NZ * NX * rows_dev
    entropic = 0.4 / math.sqrt(dims_total)

    r_id, d_id = lax.axis_index("rows"), lax.axis_index("dims")
    z, x = r_id // NX, lax.rem(r_id, NX)
    y, c = d_id // NC, lax.rem(d_id, NC)
    other = NC - 1 - c
    me_xy = x * NY + y

    def at(x_, y_, z_, c_):
        return (z_ * NX + x_, y_ * NC + c_)

    def copy(src, dst, send, recv, to):
        return pltpu.make_async_remote_copy(
            src_ref=src, dst_ref=dst, send_sem=send, recv_sem=recv, device_id=to, device_id_type=MESH
        )

    here = at(x, y, z, c)

    def xy_peer(o):
        return lax.rem(x + o // NY, NX), lax.rem(y + lax.rem(o, NY), NY)

    fetch = pltpu.make_async_copy(y_ref, ybuf, own_sem.at[1])
    fetch.start()

    barrier = pltpu.get_barrier_semaphore()

    def greet(to):
        pl.semaphore_signal(barrier, inc=1, device_id=to, device_id_type=MESH)

    for o in range(1, NX):
        greet(at(lax.rem(x + o, NX), y, z, c))
    for o in range(1, NY):
        greet(at(x, lax.rem(y + o, NY), z, c))
    greet(at(x, y, lax.rem(z + 1, NZ), c))
    greet(at(x, y, lax.rem(z + NZ - 1, NZ), c))
    greet(at(x, y, z, other))

    fetch.wait()
    wide = ybuf[...].astype(F32)
    for q in range(NX):
        lo = wide[16:24, q * quarter : q * quarter + half]
        hi = wide[16:24, q * quarter + half : (q + 1) * quarter]
        ysend[q, :, 0:quarter] = wide[0:16, q * quarter : (q + 1) * quarter].astype(BF16)
        ysend[q, :, quarter:] = jnp.concatenate([lo, hi], axis=0).astype(BF16)

    pl.semaphore_wait(barrier, (NX - 1) + (NY - 1) + 2 + 1)

    def y_copy(o):
        xt = lax.rem(x + o, NX)
        return copy(ysend.at[xt], yr.at[x], y_s.at[o - 1], y_r.at[o - 1], at(xt, y, z, c))

    x_piece = 16

    def x_copy(o, k=None):
        xt = lax.rem(x + o, NX)
        cols = pl.ds(pl.multiple_of(xt * quarter, quarter), quarter)
        rows = pl.ds(0, rows_dev) if k is None else pl.ds(k * x_piece, x_piece)
        return copy(x_ref.at[rows, cols], xg.at[x, rows], x_s.at[o - 1], x_r.at[o - 1], at(xt, y, z, c))

    for o in range(1, NX):
        y_copy(o).start()
    own_x = pltpu.make_async_copy(
        x_ref.at[:, pl.ds(pl.multiple_of(x * quarter, quarter), quarter)], xg.at[x], own_sem.at[0]
    )
    own_x.start()
    yr[x] = ysend[x]
    for o in range(1, NX):
        y_copy(o).wait()

    mid = z
    pieces = []
    for k in range(NX):
        rows = yr[k].astype(F32)
        pieces.append(rows[:, 0:quarter])
        pieces.append(jnp.concatenate([rows[0:8, quarter:], rows[8:16, quarter:]], axis=1))
    yg[mid] = jnp.concatenate(pieces, axis=0).astype(BF16)

    ahead = (at(x, y, lax.rem(z + 1, NZ), c), at(x, y, lax.rem(z + NZ - 1, NZ), c))

    def ring_copy(way, step, u, place):
        ref = yg.at[place, pl.ds(pl.multiple_of(u * piece, piece), piece)]
        return copy(ref, ref, ring_s.at[way, step - 1, u], ring_r.at[way, step - 1, u], ahead[way])

    def origins(step):
        return lax.rem(z + NZ - step, NZ), lax.rem(z + step, NZ)

    last = NZ // 2

    def ring_first(u, _):
        for way in range(2):
            ring_copy(way, 1, u, mid).start()
        return 0

    lax.fori_loop(0, PIECES, ring_first, 0)

    def pass_on(step, u, places, ways=(0, 1)):
        for way in range(2):
            ring_copy(way, step, u, places[way]).wait_recv()
            if way in ways:
                ring_copy(way, step + 1, u, places[way]).start()

    def source(b):
        away = (b + 1) // 2
        return lax.rem(jnp.where(lax.rem(b, 2) == 1, z + away, z + NZ - away), NZ)

    def core_copy(s):
        return copy(part.at[s, other], cx.at[s], core_s.at[s], core_r.at[s], at(x, y, z, other))

    def distance(b):
        s = source(b)
        rows = yg[s]
        noise_block = xg[...].reshape(NX * rows_dev, quarter)
        products = lax.dot_general(rows, noise_block, (((1,), (1,)), ((), ())), preferred_element_type=F32)
        tall = rows.astype(F32)
        data_sq = jnp.sum(tall * tall, axis=1, keepdims=True)
        value = (x2[0:1, :] + data_sq - 2.0 * products) * (1.0 / dims_total)
        for k in range(NC):
            part[s, k] = value[k * own_rows : (k + 1) * own_rows]
        core_copy(s).start()

    def sum_copy(zs, o, h):
        xt, q = lax.rem(x + o, NX), zs // pairs
        return copy(
            sm.at[zs, xt, h], rs.at[q, me_xy], sum_s.at[zs, o, h], sum_r.at[q],
            at(xt, SPLIT * lax.rem(zs, pairs) + h, z, c),
        )

    def hand_out(b):
        zs = source(b)
        core_copy(zs).wait()
        value = part[zs, c] + cx[zs]
        for k in range(NX):
            for h in range(SPLIT):
                sm[zs, k, h] = value[h * share : (h + 1) * share, k * rows_dev : (k + 1) * rows_dev]
        for o in range(1, NX):
            for h in range(SPLIT):
                sum_copy(zs, o, h).start()
        for h in range(SPLIT):
            @pl.when(SPLIT * lax.rem(zs, pairs) + h == y)
            def _():
                rs[zs // pairs, me_xy] = sm[zs, x, h]

            @pl.when(SPLIT * lax.rem(zs, pairs) + h != y)
            def _():
                sum_copy(zs, 0, h).start()

    x_turns = rows_dev // x_piece
    for k in range(max(x_turns, (LAG - 1) * PIECES)):
        if k < x_turns:
            for o in range(1, NX):
                x_copy(o, k).start()
        if k < (LAG - 1) * PIECES:
            pass_on(1 + k // PIECES, k % PIECES, origins(1 + k // PIECES))

    own_x.wait()
    for o in range(1, NX):
        x_copy(o).wait()
    for s in range(NX):
        tall = xg[s].astype(F32)
        norm = jnp.sum(tall * tall, axis=1, keepdims=True)
        flat = jnp.transpose(jnp.broadcast_to(norm, (rows_dev, rows_dev)))
        x2[:, s * rows_dev : (s + 1) * rows_dev] = flat[0:8]

    blocks = NZ - 1
    per = PIECES // 2

    def work(step, i):
        b = (step - LAG) * per + i - 1

        @pl.when((b >= 0) & (b < blocks))
        def _():
            distance(b)

        @pl.when((b >= per) & (b - per < blocks))
        def _():
            hand_out(b - per)

    def later(step, _):
        places = origins(step)

        def each(i, _):
            pass_on(step, 2 * i, places)
            pass_on(step, 2 * i + 1, places)
            work(step, i)
            return 0

        return lax.fori_loop(0, per, each, 0)

    lax.fori_loop(LAG, last - 1, later, 0)
    places = origins(last - 1)
    for i in range(per):
        for u in (2 * i, 2 * i + 1):
            pass_on(last - 1, u, places, (0,) if u < PIECES // 2 else (1,))
        work(last - 1, i)
    far = lax.rem(z + last, NZ)

    def ring_last(i, _):
        ring_copy(0, last, i, far).wait_recv()
        ring_copy(1, last, i + per, far).wait_recv()
        work(last, i)
        return 0

    lax.fori_loop(0, per, ring_last, 0)
    done = (last + 1 - LAG) * per - 1

    def rest(b, _):
        hand_out(b)
        return 0

    def rest_distance(b, _):
        distance(b)
        return 0

    lax.fori_loop(min(done, blocks), blocks, rest_distance, 0)
    distance(NZ - 1)
    lax.fori_loop(max(min(done - per, blocks), 0), blocks, rest, 0)
    hand_out(NZ - 1)

    def sum_up(b, _):
        zs = source(b)

        @pl.when(lax.rem(zs, pairs) == y // SPLIT)
        def _():
            q = zs // pairs

            others = rs.at[q, pl.ds(0, NX * NY - 1)]
            copy(others, others, sum_s.at[0, 0, 0], sum_r.at[q], here).wait_recv()
            total = rs[q, 0]
            for src in range(1, NX * NY):
                total = total + rs[q, src]
            a1[pl.ds(pl.multiple_of(q * share, 8), share), :] = total * (-1.0 / entropic)

        return 0

    lax.fori_loop(0, NZ, sum_up, 0)

    def sent_so_far():
        def ring_sent(step, _):
            def each(u, _):
                for way in range(2):
                    @pl.when((step < last) | ((u < PIECES // 2) == (way == 0)))
                    def _():
                        ring_copy(way, step, u, mid).wait_send()
                return 0

            return lax.fori_loop(0, PIECES, each, 0)

        def sums_sent(zs, _):
            for h in range(SPLIT):
                for o in range(1, NX):
                    sum_copy(zs, o, h).wait_send()

                @pl.when(SPLIT * lax.rem(zs, pairs) + h != y)
                def _():
                    sum_copy(zs, 0, h).wait_send()

            return 0

        lax.fori_loop(1, last + 1, ring_sent, 0)
        lax.fori_loop(0, NZ, sums_sent, 0)

    if padded > mine:
        a1[mine:padded, :] = jnp.full((padded - mine, rows_dev), NEG, F32)
    for h in range(padded // rows_dev):
        cut = slice(h * rows_dev, (h + 1) * rows_dev)
        a2[:, cut] = jnp.transpose(a1[cut, :])
    pb[...] = jnp.zeros_like(pb)

    def exchange(buf, it, me, n, peer, send, recv, beside=lambda: None):
        def begin(i, _):
            copy(buf.at[it, me], buf.at[it, me], send.at[it], recv.at[it], peer(lax.rem(me + i, n))).start()
            return 0

        lax.fori_loop(1, n, begin, 0, unroll=UNROLL)
        beside()
        others = buf.at[it, pl.ds(0, n - 1)]
        whole = copy(others, others, send.at[it], recv.at[it], here)
        whole.wait_recv()
        whole.wait_send()
        return buf[it]

    def yc_peer(k):
        return at(x, k // NC, z, lax.rem(k, NC))

    def row_total(it):
        rbuf[it, d_id] = logsumexp0(a1[...] + pb[...])
        return logsumexp0(exchange(rbuf, it, d_id, NY * NC, yc_peer, row_s, row_r))[0]

    full[c, x, y] = a1[0:mine, :]
    plane = ((NY, y, NX, x), (NX, x, NY, y))

    def peer_of(core, along_first, o):
        if (core == 0) == along_first:
            return at(x, lax.rem(y + o, NY), z, c)
        return at(lax.rem(x + o, NX), y, z, c)

    def one_copy(core, o, back):
        n, pos = plane[core][0:2]
        src = lax.rem(pos + n - o, n) if back else pos
        ref = full.at[0, x, src] if core == 0 else full.at[1, src, y]
        return copy(ref, ref, one_s.at[o - 1], one_r.at[o - 1], peer_of(core, True, o))

    def set_ref(core, o):
        n, pos = plane[core][2:4]
        src = lax.rem(pos + n - o, n)
        return full.at[0, src] if core == 0 else full.at[1, :, src]

    def set_copy(core, o, back):
        ref = set_ref(core, o if back else 0)
        return copy(ref, ref, set_s.at[o - 1], set_r.at[o - 1], peer_of(core, False, o))

    def over_copy(core, o):
        ref = set_ref(core, o)
        return copy(ref, ref, core2_s.at[o], core2_r.at[o], at(x, y, z, other))

    def by_core(step):
        for core in range(NC):
            @pl.when(c == core)
            def _():
                step(core)

    def near(n):
        return sorted({1, n - 1})

    def distant(n):
        return range(2, n - 1)

    def first_part(core):
        for o in range(1, plane[core][0]):
            one_copy(core, o, False).start()

    def second_part(core):
        for o in range(1, plane[core][0]):
            one_copy(core, o, True).wait_recv()
        for o in near(plane[core][2]):
            set_copy(core, o, False).start()
        over_copy(core, 0).start()

    def third_part(core):
        for o in distant(plane[core][2]):
            set_copy(core, o, False).start()
        for o in near(plane[core][2]):
            set_copy(core, o, True).wait_recv()
            over_copy(core, o).start()

    def last_part(core):
        for o in distant(plane[core][2]):
            set_copy(core, o, True).wait_recv()
            over_copy(core, o).start()

    def all_in(core):
        for o in range(plane[1 - core][2]):
            over_copy(1 - core, o).wait_recv()

    def all_out(core):
        for o in range(1, plane[core][0]):
            one_copy(core, o, False).wait_send()
        for o in range(1, plane[core][2]):
            set_copy(core, o, False).wait_send()
        for o in range(plane[core][2]):
            over_copy(core, o).wait_send()

    def spread_scores(it):
        for k, part_of in enumerate((first_part, second_part, third_part)):
            @pl.when(it == k)
            def _():
                by_core(part_of)
                if k == 0:
                    sent_so_far()

    real = lax.broadcasted_iota(jnp.int32, (1, padded), 1) < mine

    def columns_here(it):
        row = spread(math.log(columns) - row_total(it), rows_dev)
        return jnp.concatenate(
            [logsumexp0(a2[:, h : h + rows_dev] + row) for h in range(0, padded, rows_dev)], axis=1
        )

    def iteration(it, _):
        zbuf[it, r_id] = columns_here(it)
        total = logsumexp0(
            exchange(zbuf, it, r_id, NZ * NX, lambda k: (k, d_id), cz_s, cz_r, lambda: spread_scores(it))
        )[0]
        p = jnp.where(real, math.log(noise) - total, 0.0)
        for h in range(padded // rows_dev):
            cut = slice(h * rows_dev, (h + 1) * rows_dev)
            pb[cut, :] = spread(p[:, cut], rows_dev)
        return 0

    lax.fori_loop(0, ITERS - 1, iteration, 0)

    me_plane = x * NY * NC + d_id
    xbuf[0, z] = columns_here(ITERS - 1)
    pbuf[0, me_plane] = logsumexp0(
        exchange(
            xbuf, 0, z, NZ, lambda k: at(x, y, k, c), cx_s, cx_r, lambda: spread_scores(ITERS - 1)
        )
    )[0]
    found = exchange(
        pbuf, 0, me_plane, NX * NY * NC, lambda k: (z * NX + k // (NY * NC), lax.rem(k, NY * NC)),
        pot_s, pot_r, lambda: by_core(last_part),
    )
    pots = math.log(noise) - logsumexp0(found.reshape(NX, NY * NC, 1, padded))[0]
    for k in range(NY * NC):
        for h in range(padded // rows_dev):
            lo, hi = h * rows_dev, min((h + 1) * rows_dev, mine)
            pall[k % NC * NY + k // NC, lo:hi, :] = spread(pots[k, :, lo : lo + rows_dev], rows_dev)[0 : hi - lo]

    by_core(all_in)

    def t_copy(o, h):
        xt = lax.rem(x + o, NX)
        cols = pl.ds(pl.multiple_of(x * quarter + h * half, half), half)
        return copy(tst.at[o, h], t_ref.at[:, cols], t_s.at[o, h], t_r.at[o, h], at(xt, y, z, c))

    def target(i, _):
        o = lax.rem(NX // 2 + i, NX)
        xs = lax.rem(x + o, NX)
        scores = jnp.concatenate([full[k, xs] for k in range(NC)], axis=0) + pall[...]
        top = jnp.max(jnp.max(scores, axis=0), axis=0, keepdims=True)
        powers = jnp.exp(scores - top)
        weights = powers * (1.0 / jnp.sum(jnp.sum(powers, axis=0), axis=0, keepdims=True))
        for k in range(NC):
            for pair in range(pairs):
                both = [weights[k * NY + SPLIT * pair + h].reshape(nq, share, rows_dev) for h in range(SPLIT)]
                wt[:, pair, k] = jnp.concatenate(both, axis=1).astype(BF16)
        w = wt[...].reshape(columns, rows_dev)
        for h in range(2):
            value = lax.dot_general(
                w, yg[:, :, h * half : (h + 1) * half].reshape(columns, half), (((0,), (0,)), ((), ())),
                preferred_element_type=F32,
            ).astype(BF16)

            @pl.when(o > 0)
            def _():
                tst[o, h] = value
                t_copy(o, h).start()

            @pl.when(o == 0)
            def _():
                t_ref[:, pl.ds(pl.multiple_of(x * quarter + h * half, half), half)] = value

        return 0

    lax.fori_loop(0, NX, target, 0)

    ordered = [
        pots[(SPLIT * pair + h) * NC + k, :, q * share : (q + 1) * share]
        for q in range(nq) for pair in range(pairs) for k in range(NC) for h in range(SPLIT)
    ]
    pot_ref[...] = (jnp.concatenate(ordered, axis=1) * entropic).reshape(columns)
    by_core(all_out)
    for o in range(1, NX):
        for h in range(2):
            t_copy(o, h).wait()


def on_device(noise_latents, data_latents):
    rows_dev, width = noise_latents.shape
    quarter = width // NX
    block_rows = NX * 24
    own_rows = block_rows // NC
    pairs = NY // SPLIT
    nq = NZ // pairs
    share = own_rows // SPLIT
    mine = nq * share
    padded = -(-mine // rows_dev) * rows_dev
    nd = NY * NC
    dma = pltpu.SemaphoreType.DMA
    last = NZ // 2
    longest = max(NX, NY)
    sems = [
        (NX - 1,), (NX - 1,), (NX - 1,), (NX - 1,), (2,),
        (2, last, PIECES), (2, last, PIECES), (NZ,), (NZ,), (NZ, NX, SPLIT), (nq,),
        (ITERS,), (ITERS,), (ITERS - 1,), (ITERS - 1,), (1,), (1,),
        (1,), (1,),
        (longest,), (longest,), (longest,), (longest,), (longest,), (longest,), (NX, 2), (NX, 2),
    ]
    targets, pots = pl.pallas_call(
        functools.partial(kernel, width * nd),
        out_shape=(
            pltpu.VMEM((rows_dev, width), BF16),
            jax.ShapeDtypeStruct((NZ * block_rows,), F32),
        ),
        in_specs=[pl.BlockSpec(memory_space=pl.ANY)] * 2,
        out_specs=(pl.BlockSpec(memory_space=pltpu.VMEM),) * 2,
        scratch_shapes=[
            pltpu.VMEM(data_latents.shape, BF16),
            pltpu.VMEM((NX, 16, quarter * 3 // 2), BF16),
            pltpu.VMEM((NX, 16, quarter * 3 // 2), BF16),
            pltpu.VMEM((NX, rows_dev, quarter), BF16),
            pltpu.VMEM((NZ, block_rows, quarter), BF16),
            pltpu.VMEM((8, NX * rows_dev), F32),
            pltpu.VMEM((NZ, NC, own_rows, NX * rows_dev), F32),
            pltpu.VMEM((NZ, own_rows, NX * rows_dev), F32),
            pltpu.VMEM((NZ, NX, SPLIT, share, rows_dev), F32),
            pltpu.VMEM((nq, NX * NY, share, rows_dev), F32),
            pltpu.VMEM((padded, rows_dev), F32),
            pltpu.VMEM((rows_dev, padded), F32),
            pltpu.VMEM((padded, rows_dev), F32),
            pltpu.VMEM((ITERS, nd, 1, rows_dev), F32),
            pltpu.VMEM((ITERS - 1, NZ * NX, 1, padded), F32),
            pltpu.VMEM((1, NZ, 1, padded), F32),
            pltpu.VMEM((1, NX * nd, 1, padded), F32),
            pltpu.VMEM((NC, NX, NY, mine, rows_dev), F32),
            pltpu.VMEM((nd, mine, rows_dev), F32),
            pltpu.VMEM((nq, pairs, NC, own_rows, rows_dev), BF16),
            pltpu.VMEM((NX, 2, rows_dev, quarter // 2), BF16),
        ]
        + [dma(shape) for shape in sems],
        compiler_params=pltpu.CompilerParams(
            collective_id=0, has_side_effects=True, vmem_limit_bytes=60 * 1024 * 1024
        ),
    )(noise_latents, data_latents)
    return targets, pots


def solution(mesh):
    placed = (P("rows", "dims"), P("rows", "dims"))
    return jax.shard_map(
        on_device, mesh=mesh, in_specs=placed, out_specs=(P("rows", "dims"), P()), check_vma=False
    )
```

```python
import functools
import math

import jax
import jax.numpy as jnp
from jax import lax
from jax.experimental import pallas as pl
from jax.experimental.pallas import tpu as pltpu
from jax.sharding import PartitionSpec as P

ITERS = 3
NZ, NX, NY, NC = 16, 4, 4, 2
PIECES = 6
SPLIT = 1
UNROLL = 3
LAG = 3
NEG = -1e30
MESH = pl.DeviceIdType.MESH
F32, BF16 = jnp.float32, jnp.bfloat16


def logsumexp0(v):
    top = jnp.max(v, axis=0, keepdims=True)
    return top + jnp.log(jnp.sum(jnp.exp(v - top), axis=0, keepdims=True))


def spread(v, n):
    return jnp.transpose(jnp.broadcast_to(v, (n, n)))


def kernel(
    dims_total, x_ref, y_ref, t_ref, pot_ref,
    ysend, yr, xg, yg, x2, part, cx, sm, rs, a1, a2, pb, rbuf, zbuf, xbuf, pbuf, full, pall, wt, tst,
    y_s, y_r, x_s, x_r, own_sem, ring_s, ring_r, core_s, core_r, sum_s, sum_r,
    row_s, row_r, cz_s, cz_r, cx_s, cx_r, pot_s, pot_r, one_s, one_r, set_s, set_r, core2_s, core2_r, t_s, t_r,
):
    rows_dev, width = x_ref.shape
    quarter = width // NX
    half = quarter // 2
    block_rows = NX * 24
    own_rows = block_rows // NC
    pairs = NY // SPLIT
    nq = NZ // pairs
    share = own_rows // SPLIT
    mine = nq * share
    padded = a1.shape[0]
    piece = block_rows // PIECES
    columns = NZ * block_rows
    noise = NZ * NX * rows_dev
    entropic = 0.4 / math.sqrt(dims_total)

    r_id, d_id = lax.axis_index("rows"), lax.axis_index("dims")
    z, x = r_id // NX, lax.rem(r_id, NX)
    y, c = d_id // NC, lax.rem(d_id, NC)
    other = NC - 1 - c
    me_xy = x * NY + y

    def at(x_, y_, z_, c_):
        return (z_ * NX + x_, y_ * NC + c_)

    def copy(src, dst, send, recv, to):
        return pltpu.make_async_remote_copy(
            src_ref=src, dst_ref=dst, send_sem=send, recv_sem=recv, device_id=to, device_id_type=MESH
        )

    here = at(x, y, z, c)

    def xy_peer(o):
        return lax.rem(x + o // NY, NX), lax.rem(y + lax.rem(o, NY), NY)

    barrier = pltpu.get_barrier_semaphore()

    def greet(to):
        pl.semaphore_signal(barrier, inc=1, device_id=to, device_id_type=MESH)

    for o in range(1, NX):
        greet(at(lax.rem(x + o, NX), y, z, c))
    for o in range(1, NY):
        greet(at(x, lax.rem(y + o, NY), z, c))
    greet(at(x, y, lax.rem(z + 1, NZ), c))
    greet(at(x, y, lax.rem(z + NZ - 1, NZ), c))
    greet(at(x, y, z, other))

    wide = y_ref[...].astype(F32)
    for q in range(NX):
        lo = wide[16:24, q * quarter : q * quarter + half]
        hi = wide[16:24, q * quarter + half : (q + 1) * quarter]
        ysend[q, :, 0:quarter] = wide[0:16, q * quarter : (q + 1) * quarter].astype(BF16)
        ysend[q, :, quarter:] = jnp.concatenate([lo, hi], axis=0).astype(BF16)

    pl.semaphore_wait(barrier, (NX - 1) + (NY - 1) + 2 + 1)

    def y_copy(o):
        xt = lax.rem(x + o, NX)
        return copy(ysend.at[xt], yr.at[x], y_s.at[o - 1], y_r.at[o - 1], at(xt, y, z, c))

    x_piece = 16

    def x_copy(o, k=None):
        xt = lax.rem(x + o, NX)
        cols = pl.ds(pl.multiple_of(xt * quarter, quarter), quarter)
        rows = pl.ds(0, rows_dev) if k is None else pl.ds(k * x_piece, x_piece)
        return copy(x_ref.at[rows, cols], xg.at[x, rows], x_s.at[o - 1], x_r.at[o - 1], at(xt, y, z, c))

    for o in range(1, NX):
        y_copy(o).start()
    own_x = pltpu.make_async_copy(
        x_ref.at[:, pl.ds(pl.multiple_of(x * quarter, quarter), quarter)], xg.at[x], own_sem.at[0]
    )
    own_x.start()
    yr[x] = ysend[x]
    for o in range(1, NX):
        y_copy(o).wait()

    mid = z
    pieces = []
    for k in range(NX):
        rows = yr[k].astype(F32)
        pieces.append(rows[:, 0:quarter])
        pieces.append(jnp.concatenate([rows[0:8, quarter:], rows[8:16, quarter:]], axis=1))
    yg[mid] = jnp.concatenate(pieces, axis=0).astype(BF16)

    ahead = (at(x, y, lax.rem(z + 1, NZ), c), at(x, y, lax.rem(z + NZ - 1, NZ), c))

    def ring_copy(way, step, u, place):
        ref = yg.at[place, pl.ds(pl.multiple_of(u * piece, piece), piece)]
        return copy(ref, ref, ring_s.at[way, step - 1, u], ring_r.at[way, step - 1, u], ahead[way])

    def origins(step):
        return lax.rem(z + NZ - step, NZ), lax.rem(z + step, NZ)

    last = NZ // 2

    def ring_first(u, _):
        for way in range(2):
            ring_copy(way, 1, u, mid).start()
        return 0

    lax.fori_loop(0, PIECES, ring_first, 0)

    def pass_on(step, u, places, ways=(0, 1)):
        for way in range(2):
            ring_copy(way, step, u, places[way]).wait_recv()
            if way in ways:
                ring_copy(way, step + 1, u, places[way]).start()

    def source(b):
        away = (b + 1) // 2
        return lax.rem(jnp.where(lax.rem(b, 2) == 1, z + away, z + NZ - away), NZ)

    def core_copy(s):
        return copy(part.at[s, other], cx.at[s], core_s.at[s], core_r.at[s], at(x, y, z, other))

    def distance(b):
        s = source(b)
        rows = yg[s]
        noise_block = xg[...].reshape(NX * rows_dev, quarter)
        products = lax.dot_general(rows, noise_block, (((1,), (1,)), ((), ())), preferred_element_type=F32)
        tall = rows.astype(F32)
        data_sq = jnp.sum(tall * tall, axis=1, keepdims=True)
        value = (x2[0:1, :] + data_sq - 2.0 * products) * (1.0 / dims_total)
        for k in range(NC):
            part[s, k] = value[k * own_rows : (k + 1) * own_rows]
        core_copy(s).start()

    def sum_copy(zs, o, h):
        xt, q = lax.rem(x + o, NX), zs // pairs
        return copy(
            sm.at[zs, xt, h], rs.at[q, me_xy], sum_s.at[zs, o, h], sum_r.at[q],
            at(xt, SPLIT * lax.rem(zs, pairs) + h, z, c),
        )

    def hand_out(b):
        zs = source(b)
        core_copy(zs).wait()
        value = part[zs, c] + cx[zs]
        for k in range(NX):
            for h in range(SPLIT):
                sm[zs, k, h] = value[h * share : (h + 1) * share, k * rows_dev : (k + 1) * rows_dev]
        for o in range(1, NX):
            for h in range(SPLIT):
                sum_copy(zs, o, h).start()
        for h in range(SPLIT):
            @pl.when(SPLIT * lax.rem(zs, pairs) + h == y)
            def _():
                rs[zs // pairs, me_xy] = sm[zs, x, h]

            @pl.when(SPLIT * lax.rem(zs, pairs) + h != y)
            def _():
                sum_copy(zs, 0, h).start()

    x_turns = rows_dev // x_piece
    for k in range(max(x_turns, (LAG - 1) * PIECES)):
        if k < x_turns:
            for o in range(1, NX):
                x_copy(o, k).start()
        if k < (LAG - 1) * PIECES:
            pass_on(1 + k // PIECES, k % PIECES, origins(1 + k // PIECES))

    own_x.wait()
    for o in range(1, NX):
        x_copy(o).wait()
    for s in range(NX):
        tall = xg[s].astype(F32)
        norm = jnp.sum(tall * tall, axis=1, keepdims=True)
        flat = jnp.transpose(jnp.broadcast_to(norm, (rows_dev, rows_dev)))
        x2[:, s * rows_dev : (s + 1) * rows_dev] = flat[0:8]

    blocks = NZ - 1
    per = PIECES // 2

    def work(step, i):
        b = (step - LAG) * per + i - 1

        @pl.when((b >= 0) & (b < blocks))
        def _():
            distance(b)

        @pl.when((b >= per) & (b - per < blocks))
        def _():
            hand_out(b - per)

    def later(step, _):
        places = origins(step)

        def each(i, _):
            pass_on(step, 2 * i, places)
            pass_on(step, 2 * i + 1, places)
            work(step, i)
            return 0

        return lax.fori_loop(0, per, each, 0)

    lax.fori_loop(LAG, last - 1, later, 0)
    places = origins(last - 1)
    for i in range(per):
        for u in (2 * i, 2 * i + 1):
            pass_on(last - 1, u, places, (0,) if u < PIECES // 2 else (1,))
        work(last - 1, i)
    far = lax.rem(z + last, NZ)

    def ring_last(i, _):
        ring_copy(0, last, i, far).wait_recv()
        ring_copy(1, last, i + per, far).wait_recv()
        work(last, i)
        return 0

    lax.fori_loop(0, per, ring_last, 0)
    done = (last + 1 - LAG) * per - 1

    def rest(b, _):
        hand_out(b)
        return 0

    def rest_distance(b, _):
        distance(b)
        return 0

    lax.fori_loop(min(done, blocks), blocks, rest_distance, 0)
    distance(NZ - 1)
    lax.fori_loop(max(min(done - per, blocks), 0), blocks, rest, 0)
    hand_out(NZ - 1)

    def sum_up(b, _):
        zs = source(b)

        @pl.when(lax.rem(zs, pairs) == y // SPLIT)
        def _():
            q = zs // pairs

            others = rs.at[q, pl.ds(0, NX * NY - 1)]
            copy(others, others, sum_s.at[0, 0, 0], sum_r.at[q], here).wait_recv()
            total = rs[q, 0]
            for src in range(1, NX * NY):
                total = total + rs[q, src]
            a1[pl.ds(pl.multiple_of(q * share, 8), share), :] = total * (-1.0 / entropic)

        return 0

    lax.fori_loop(0, NZ, sum_up, 0)

    def sent_so_far():
        def ring_sent(step, _):
            def each(u, _):
                for way in range(2):
                    @pl.when((step < last) | ((u < PIECES // 2) == (way == 0)))
                    def _():
                        ring_copy(way, step, u, mid).wait_send()
                return 0

            return lax.fori_loop(0, PIECES, each, 0)

        def sums_sent(zs, _):
            for h in range(SPLIT):
                for o in range(1, NX):
                    sum_copy(zs, o, h).wait_send()

                @pl.when(SPLIT * lax.rem(zs, pairs) + h != y)
                def _():
                    sum_copy(zs, 0, h).wait_send()

            return 0

        lax.fori_loop(1, last + 1, ring_sent, 0)
        lax.fori_loop(0, NZ, sums_sent, 0)

    if padded > mine:
        a1[mine:padded, :] = jnp.full((padded - mine, rows_dev), NEG, F32)
    for h in range(padded // rows_dev):
        cut = slice(h * rows_dev, (h + 1) * rows_dev)
        a2[:, cut] = jnp.transpose(a1[cut, :])
    pb[...] = jnp.zeros_like(pb)

    def exchange(buf, it, me, n, peer, send, recv, beside=lambda: None):
        def begin(i, _):
            copy(buf.at[it, me], buf.at[it, me], send.at[it], recv.at[it], peer(lax.rem(me + i, n))).start()
            return 0

        lax.fori_loop(1, n, begin, 0, unroll=UNROLL)
        beside()
        others = buf.at[it, pl.ds(0, n - 1)]
        whole = copy(others, others, send.at[it], recv.at[it], here)
        whole.wait_recv()
        whole.wait_send()
        return buf[it]

    def yc_peer(k):
        return at(x, k // NC, z, lax.rem(k, NC))

    def row_total(it):
        rbuf[it, d_id] = logsumexp0(a1[...] + pb[...])
        return logsumexp0(exchange(rbuf, it, d_id, NY * NC, yc_peer, row_s, row_r))[0]

    full[c, x, y] = a1[0:mine, :]
    plane = ((NY, y, NX, x), (NX, x, NY, y))

    def peer_of(core, along_first, o):
        if (core == 0) == along_first:
            return at(x, lax.rem(y + o, NY), z, c)
        return at(lax.rem(x + o, NX), y, z, c)

    def one_copy(core, o, back):
        n, pos = plane[core][0:2]
        src = lax.rem(pos + n - o, n) if back else pos
        ref = full.at[0, x, src] if core == 0 else full.at[1, src, y]
        return copy(ref, ref, one_s.at[o - 1], one_r.at[o - 1], peer_of(core, True, o))

    def set_ref(core, o):
        n, pos = plane[core][2:4]
        src = lax.rem(pos + n - o, n)
        return full.at[0, src] if core == 0 else full.at[1, :, src]

    def set_copy(core, o, back):
        ref = set_ref(core, o if back else 0)
        return copy(ref, ref, set_s.at[o - 1], set_r.at[o - 1], peer_of(core, False, o))

    def over_copy(core, o):
        ref = set_ref(core, o)
        return copy(ref, ref, core2_s.at[o], core2_r.at[o], at(x, y, z, other))

    def by_core(step):
        for core in range(NC):
            @pl.when(c == core)
            def _():
                step(core)

    def near(n):
        return sorted({1, n - 1})

    def distant(n):
        return range(2, n - 1)

    def first_part(core):
        for o in range(1, plane[core][0]):
            one_copy(core, o, False).start()

    def second_part(core):
        for o in range(1, plane[core][0]):
            one_copy(core, o, True).wait_recv()
        for o in near(plane[core][2]):
            set_copy(core, o, False).start()
        over_copy(core, 0).start()

    def third_part(core):
        for o in distant(plane[core][2]):
            set_copy(core, o, False).start()
        for o in near(plane[core][2]):
            set_copy(core, o, True).wait_recv()
            over_copy(core, o).start()

    def last_part(core):
        for o in distant(plane[core][2]):
            set_copy(core, o, True).wait_recv()
            over_copy(core, o).start()

    def all_in(core):
        for o in range(plane[1 - core][2]):
            over_copy(1 - core, o).wait_recv()

    def all_out(core):
        for o in range(1, plane[core][0]):
            one_copy(core, o, False).wait_send()
        for o in range(1, plane[core][2]):
            set_copy(core, o, False).wait_send()
        for o in range(plane[core][2]):
            over_copy(core, o).wait_send()

    def spread_scores(it):
        for k, part_of in enumerate((first_part, second_part, third_part)):
            @pl.when(it == k)
            def _():
                by_core(part_of)
                if k == 0:
                    sent_so_far()

    real = lax.broadcasted_iota(jnp.int32, (1, padded), 1) < mine

    def columns_here(it):
        row = spread(math.log(columns) - row_total(it), rows_dev)
        return jnp.concatenate(
            [logsumexp0(a2[:, h : h + rows_dev] + row) for h in range(0, padded, rows_dev)], axis=1
        )

    def iteration(it, _):
        zbuf[it, r_id] = columns_here(it)
        total = logsumexp0(
            exchange(zbuf, it, r_id, NZ * NX, lambda k: (k, d_id), cz_s, cz_r, lambda: spread_scores(it))
        )[0]
        p = jnp.where(real, math.log(noise) - total, 0.0)
        for h in range(padded // rows_dev):
            cut = slice(h * rows_dev, (h + 1) * rows_dev)
            pb[cut, :] = spread(p[:, cut], rows_dev)
        return 0

    lax.fori_loop(0, ITERS - 1, iteration, 0)

    me_plane = x * NY * NC + d_id
    xbuf[0, z] = columns_here(ITERS - 1)
    pbuf[0, me_plane] = logsumexp0(
        exchange(
            xbuf, 0, z, NZ, lambda k: at(x, y, k, c), cx_s, cx_r, lambda: spread_scores(ITERS - 1)
        )
    )[0]
    found = exchange(
        pbuf, 0, me_plane, NX * NY * NC, lambda k: (z * NX + k // (NY * NC), lax.rem(k, NY * NC)),
        pot_s, pot_r, lambda: by_core(last_part),
    )
    pots = math.log(noise) - logsumexp0(found.reshape(NX, NY * NC, 1, padded))[0]
    for k in range(NY * NC):
        for h in range(padded // rows_dev):
            lo, hi = h * rows_dev, min((h + 1) * rows_dev, mine)
            pall[k % NC * NY + k // NC, lo:hi, :] = spread(pots[k, :, lo : lo + rows_dev], rows_dev)[0 : hi - lo]

    by_core(all_in)

    def t_copy(o, h):
        xt = lax.rem(x + o, NX)
        cols = pl.ds(pl.multiple_of(x * quarter + h * half, half), half)
        return copy(tst.at[o, h], t_ref.at[:, cols], t_s.at[o, h], t_r.at[o, h], at(xt, y, z, c))

    def target(i, _):
        o = lax.rem(NX // 2 + i, NX)
        xs = lax.rem(x + o, NX)
        scores = jnp.concatenate([full[k, xs] for k in range(NC)], axis=0) + pall[...]
        top = jnp.max(jnp.max(scores, axis=0), axis=0, keepdims=True)
        powers = jnp.exp(scores - top)
        weights = powers * (1.0 / jnp.sum(jnp.sum(powers, axis=0), axis=0, keepdims=True))
        for k in range(NC):
            for pair in range(pairs):
                both = [weights[k * NY + SPLIT * pair + h].reshape(nq, share, rows_dev) for h in range(SPLIT)]
                wt[:, pair, k] = jnp.concatenate(both, axis=1).astype(BF16)
        w = wt[...].reshape(columns, rows_dev)
        for h in range(2):
            value = lax.dot_general(
                w, yg[:, :, h * half : (h + 1) * half].reshape(columns, half), (((0,), (0,)), ((), ())),
                preferred_element_type=F32,
            ).astype(BF16)

            @pl.when(o > 0)
            def _():
                tst[o, h] = value
                t_copy(o, h).start()

            @pl.when(o == 0)
            def _():
                t_ref[:, pl.ds(pl.multiple_of(x * quarter + h * half, half), half)] = value

        return 0

    lax.fori_loop(0, NX, target, 0)

    ordered = [
        pots[(SPLIT * pair + h) * NC + k, :, q * share : (q + 1) * share]
        for q in range(nq) for pair in range(pairs) for k in range(NC) for h in range(SPLIT)
    ]
    pot_ref[...] = (jnp.concatenate(ordered, axis=1) * entropic).reshape(columns)
    by_core(all_out)
    for o in range(1, NX):
        for h in range(2):
            t_copy(o, h).wait()


def on_device(noise_latents, data_latents):
    rows_dev, width = noise_latents.shape
    quarter = width // NX
    block_rows = NX * 24
    own_rows = block_rows // NC
    pairs = NY // SPLIT
    nq = NZ // pairs
    share = own_rows // SPLIT
    mine = nq * share
    padded = -(-mine // rows_dev) * rows_dev
    nd = NY * NC
    dma = pltpu.SemaphoreType.DMA
    last = NZ // 2
    longest = max(NX, NY)
    sems = [
        (NX - 1,), (NX - 1,), (NX - 1,), (NX - 1,), (1,),
        (2, last, PIECES), (2, last, PIECES), (NZ,), (NZ,), (NZ, NX, SPLIT), (nq,),
        (ITERS,), (ITERS,), (ITERS - 1,), (ITERS - 1,), (1,), (1,),
        (1,), (1,),
        (longest,), (longest,), (longest,), (longest,), (longest,), (longest,), (NX, 2), (NX, 2),
    ]
    targets, pots = pl.pallas_call(
        functools.partial(kernel, width * nd),
        out_shape=(
            pltpu.VMEM((rows_dev, width), BF16),
            jax.ShapeDtypeStruct((NZ * block_rows,), F32),
        ),
        in_specs=[pl.BlockSpec(memory_space=pl.ANY), pl.BlockSpec(memory_space=pltpu.VMEM)],
        out_specs=(pl.BlockSpec(memory_space=pltpu.VMEM),) * 2,
        scratch_shapes=[
            pltpu.VMEM((NX, 16, quarter * 3 // 2), BF16),
            pltpu.VMEM((NX, 16, quarter * 3 // 2), BF16),
            pltpu.VMEM((NX, rows_dev, quarter), BF16),
            pltpu.VMEM((NZ, block_rows, quarter), BF16),
            pltpu.VMEM((8, NX * rows_dev), F32),
            pltpu.VMEM((NZ, NC, own_rows, NX * rows_dev), F32),
            pltpu.VMEM((NZ, own_rows, NX * rows_dev), F32),
            pltpu.VMEM((NZ, NX, SPLIT, share, rows_dev), F32),
            pltpu.VMEM((nq, NX * NY, share, rows_dev), F32),
            pltpu.VMEM((padded, rows_dev), F32),
            pltpu.VMEM((rows_dev, padded), F32),
            pltpu.VMEM((padded, rows_dev), F32),
            pltpu.VMEM((ITERS, nd, 1, rows_dev), F32),
            pltpu.VMEM((ITERS - 1, NZ * NX, 1, padded), F32),
            pltpu.VMEM((1, NZ, 1, padded), F32),
            pltpu.VMEM((1, NX * nd, 1, padded), F32),
            pltpu.VMEM((NC, NX, NY, mine, rows_dev), F32),
            pltpu.VMEM((nd, mine, rows_dev), F32),
            pltpu.VMEM((nq, pairs, NC, own_rows, rows_dev), BF16),
            pltpu.VMEM((NX, 2, rows_dev, quarter // 2), BF16),
        ]
        + [dma(shape) for shape in sems],
        compiler_params=pltpu.CompilerParams(
            collective_id=0, has_side_effects=True, vmem_limit_bytes=60 * 1024 * 1024
        ),
    )(noise_latents, data_latents)
    return targets, pots


def solution(mesh):
    placed = (P("rows", "dims"), P("rows", "dims"))
    return jax.shard_map(
        on_device, mesh=mesh, in_specs=placed, out_specs=(P("rows", "dims"), P()), check_vma=False
    )
```
